512 devices in a mesh: dom: 32 (over z, x), tm: 16 (over y, core).
Axes of the slice: x: 4, y: 8, z: 8, core: 2. Of those that a mesh axis runs over, the one named last changes fastest.
Arguments:
- signal: bfloat16 [8, 512, 65536], P(None, 'tm', 'dom'), may hold values from -6 to 6
- weights: bfloat16 [512, 5, 128, 128], P('dom'), may hold values from 0 to 10.5, as said below
- send_list: int32 [32, 4, 3], P('dom'), may hold values from 0 to 15, as said below
- col_ref: int32 [512, 5], P('dom'), may hold values from 0 to 27, as said below
- kernel: bfloat16 [512, 512], P('tm'), may hold values from -0.2 to 1.6
- cheb_coef: float32 [3], replicated, may hold values from 0.5 to 1.5
Outputs:
- filtered: bfloat16 [8, 512, 65536], P(None, 'tm', 'dom')
The draws below stay inside these ranges and needn't reach their ends.
Inputs may be any that keep to these rules, and one draw needn't show every extreme that they name: `send_list`: for each q and k the 3 entries are distinct block rows of partition q. col_ref[g, 0] = g % 16. An entry e >= 16 of partition p names partition q = p + d_k (k = (e - 16) // 3), which always exists; for each p and k the slots s used run from 0 up to some count of at most 3, every such slot is used by some block row of p, and some partition uses all 3 from some k. `weights`: Nonnegative; every diagonal entry of slot 0 blocks is 0.5 or more.
All inputs are finite; a program needn't handle non-finite values.
Results may differ from the reference program's by a relative error of at most 0.023.
Values may be sent and summed in bfloat16 or wider, within the bound.
No kernel may reach another device: no remote copies, remote signals or barrier semaphores. Data moves between devices by JAX's collectives and lax.ppermute only.
A program may use at most 64 MiB of HBM per device.

```python
import math
import jax
import jax.numpy as jnp
from jax import lax

PROBES = 8
TIME = 512
BLOCK = 128
NB_DEV = 16
BPR = 5
REACH = 2
SLOTS = 3
NODES = 65536
N_DOM = 32


def halo_plan(key):
    count_key, list_key, fill_key, order_key = jax.random.split(key, 4)
    ways = 2 * REACH
    part_index = jnp.arange(N_DOM, dtype=jnp.int32)[:, None]
    way_index = jnp.arange(ways, dtype=jnp.int32)[None, :]
    offsets = jnp.where(way_index < REACH, way_index - REACH, way_index - REACH + 1)
    source_part = part_index + offsets
    is_valid = (source_part >= 0) & (source_part < N_DOM)
    counts = jax.random.randint(count_key, (N_DOM, ways), 1, SLOTS + 1).astype(jnp.int32)
    counts = jnp.where(way_index == part_index % ways, SLOTS, counts)
    counts = jnp.where(is_valid, counts, 0).astype(jnp.int32)
    list_keys = jax.random.split(list_key, N_DOM * ways)
    send_list = jax.vmap(lambda one_key: jax.random.permutation(one_key, NB_DEV)[:SLOTS])(list_keys)
    send_list = send_list.reshape(N_DOM, ways, SLOTS).astype(jnp.int32)
    per_part = NB_DEV * (BPR - 1)
    flat_slot = jnp.arange(per_part, dtype=jnp.int32)[None, :]
    ref_way = jnp.minimum(flat_slot // SLOTS, ways - 1)
    ref_slot = flat_slot % SLOTS
    way_counts = jnp.take_along_axis(counts, jnp.broadcast_to(ref_way, (N_DOM, per_part)), axis=1)
    is_used = (flat_slot < ways * SLOTS) & (ref_slot < way_counts)
    local_pick = jax.random.randint(fill_key, (N_DOM, per_part), 0, NB_DEV).astype(jnp.int32)
    chosen = jnp.where(is_used, NB_DEV + flat_slot, local_pick).astype(jnp.int32)
    order_keys = jax.random.split(order_key, N_DOM)
    shuffle = jax.vmap(lambda one_key: jax.random.permutation(one_key, per_part))(order_keys).astype(jnp.int32)
    chosen = jnp.take_along_axis(chosen, shuffle, axis=1)
    rest_cols = chosen.reshape(N_DOM * NB_DEV, BPR - 1)
    own_column = (jnp.arange(N_DOM * NB_DEV, dtype=jnp.int32) % NB_DEV)[:, None]
    col_ref = jnp.concatenate([own_column, rest_cols], axis=1).astype(jnp.int32)
    return (send_list, col_ref)


def draw_send_list(key, part):
    plan_pair = halo_plan(key)
    return plan_pair[0]


def draw_col_ref(key, part):
    plan_pair = halo_plan(key)
    return plan_pair[1]


def draw_weights(key, part):
    key = jax.random.fold_in(key, 11)
    mask_key, value_key = jax.random.split(key, 2)
    full_shape = (N_DOM * NB_DEV, BPR, BLOCK, BLOCK)
    keep_mask = jax.random.uniform(mask_key, full_shape, jnp.float32) < 0.0625
    values = jnp.exp(jax.random.uniform(value_key, full_shape, jnp.float32, math.log(0.01), 0.0))
    slot_iota = lax.broadcasted_iota(jnp.int32, full_shape, 1)
    row_iota = lax.broadcasted_iota(jnp.int32, full_shape, 2)
    col_iota = lax.broadcasted_iota(jnp.int32, full_shape, 3)
    self_loop = jnp.where((slot_iota == 0) & (row_iota == col_iota), 0.5, 0.0)
    return (jnp.where(keep_mask, values, 0.0) + self_loop).astype(jnp.bfloat16)


def draw_kernel(key, part):
    key = jax.random.fold_in(key, 23)
    full_shape = (TIME, TIME)
    noise_part = jax.random.normal(key, full_shape, jnp.float32) * (0.6 / math.sqrt(TIME))
    diag_value = 1.0
    noise_part = jnp.clip(noise_part, -0.19, 0.19)
    on_diagonal = lax.broadcasted_iota(jnp.int32, full_shape, 0) == lax.broadcasted_iota(jnp.int32, full_shape, 1)
    return (noise_part + jnp.where(on_diagonal, diag_value, 0.0)).astype(jnp.bfloat16)


def block_levels(key, dims, pieces, low, top_value):
    loudness, own = 1.0, jax.random.fold_in(key, 6)
    for axis_at, blocks in pieces:
        heights = jnp.exp(jax.random.uniform(jax.random.fold_in(own, axis_at), (blocks,), jnp.float32, low / len(pieces), top_value / len(pieces)))
        loudness = loudness * jnp.repeat(heights, dims[axis_at] // blocks).reshape([-1 if axis == axis_at else 1 for axis in range(len(dims))])
    return loudness


def centred(own_key, extent, scale, bound, pieces=(), kind=jnp.bfloat16):
    values = scale * jax.random.normal(own_key, extent, jnp.float32)
    if pieces:
        values = values * block_levels(own_key, extent, pieces, -0.22, 0.18)
    return jnp.clip(values, -bound, bound).astype(kind)


def setup_inputs(seed: int = 0) -> dict:
    seeds = jax.random.split(jax.random.key(seed), 7)
    return {
        "signal": centred(seeds[0], (PROBES, TIME, NODES), 1.0, 6.0, ((1, 16), (2, 32))),
        "weights": draw_weights(jax.random.fold_in(seeds[6], 71), 0),
        "send_list": draw_send_list(jax.random.fold_in(seeds[6], 71), 0),
        "col_ref": draw_col_ref(jax.random.fold_in(seeds[6], 71), 0),
        "kernel": draw_kernel(jax.random.fold_in(seeds[6], 71), 0),
        "cheb_coef": jnp.clip(jax.random.uniform(seeds[5], (3,), jnp.float32, 0.5, 1.5), 0.5, 1.5),
    }


def reference(signal, weights, send_list, col_ref, kernel, cheb_coef):
    total_blocks = weights.shape[0]
    row_count = PROBES * TIME
    offsets = jnp.array(list(range(-REACH, 0)) + list(range(1, REACH + 1)), dtype=jnp.int32)
    owner_part = (jnp.arange(total_blocks, dtype=jnp.int32) // NB_DEV)[:, None]
    remote = jnp.maximum(col_ref - NB_DEV, 0).astype(jnp.int32)
    way_index = remote // SLOTS
    slot_index = remote % SLOTS
    source_part = jnp.clip(owner_part + offsets[way_index], 0, N_DOM - 1).astype(jnp.int32)
    sent_block = send_list[source_part, way_index, slot_index]
    global_cols = jnp.where(col_ref < NB_DEV, owner_part * NB_DEV + col_ref, source_part * NB_DEV + sent_block).astype(jnp.int32)
    degree = lax.optimization_barrier(jnp.sum(weights.astype(jnp.float32), axis=(1, 3)))
    inv_root = lax.rsqrt(degree)[:, None, :]
    signal_blocks = signal.reshape(row_count, total_blocks, BLOCK).transpose(1, 0, 2)

    def product(field):
        scaled = (field.astype(jnp.float32) * inv_root).astype(jnp.bfloat16)

        def one_block_row(inputs):
            column_ids, blocks = inputs
            picked = scaled[column_ids].astype(jnp.float32)
            return jnp.einsum('jrm,jnm->rn', picked, blocks.astype(jnp.float32))
        return lax.map(one_block_row, (global_cols, weights))
    first_sum = product(signal_blocks)
    term_one = (-inv_root * first_sum).astype(jnp.bfloat16)
    second_sum = product(term_one)
    term_two = (-2.0 * inv_root * second_sum - signal_blocks.astype(jnp.float32)).astype(jnp.bfloat16)
    mixed = (cheb_coef[0] * signal_blocks.astype(jnp.float32) + cheb_coef[1] * term_one.astype(jnp.float32) + cheb_coef[2] * term_two.astype(jnp.float32)).astype(jnp.bfloat16)
    slab_field = mixed.transpose(1, 0, 2).reshape(PROBES, TIME, total_blocks * BLOCK)
    result_field = jnp.einsum('ut,ptn->pun', kernel.astype(jnp.float32), slab_field.astype(jnp.float32))
    return result_field.astype(jnp.bfloat16)
```

```python
import functools

import jax
import jax.numpy as jnp
from jax import lax
from jax.experimental import pallas as pl
from jax.experimental.pallas import tpu as pltpu
from jax.sharding import PartitionSpec as P

REACH = 2
OFFSETS = tuple(range(-REACH, 0)) + tuple(range(1, REACH + 1))
F32, BF16 = jnp.float32, jnp.bfloat16
VMEM = pl.BlockSpec(memory_space=pltpu.VMEM)
SMEM = pl.BlockSpec(memory_space=pltpu.SMEM)
LIMIT = 24 * 2**20


def call(kernel, outs, ins, scratch=(), flops=0, name=None):
    size = sum(a.size * a.dtype.itemsize for a in (*ins, *outs))
    specs = [SMEM if a.dtype == jnp.int32 or a.size < 8 else VMEM for a in ins]
    return pl.pallas_call(
        kernel,
        out_shape=outs,
        in_specs=specs,
        out_specs=[VMEM] * len(outs),
        scratch_shapes=list(scratch),
        compiler_params=pltpu.CompilerParams(vmem_limit_bytes=LIMIT),
        cost_estimate=pl.CostEstimate(flops=flops, bytes_accessed=size, transcendentals=0),
        name=name,
    )(*ins)


def array(*shape, dtype=BF16):
    return jax.ShapeDtypeStruct(shape, dtype)


def times_transposed(a, b):
    return lax.dot_general(a, b, (((1,), (1,)), ((), ())), preferred_element_type=F32)


def pack(send_ref, field_ref, packs):
    for way, out in enumerate(packs):
        for slot in range(out.shape[0]):
            out[slot] = field_ref[send_ref[0, way, slot]]


def first_scale(signal_ref, weights_ref, send_ref, scaled_ref, inv_ref, *packs):
    blocks, per_row, width, _ = weights_ref.shape
    ones = jnp.ones((16, width), BF16)
    for g in range(blocks):
        degree = times_transposed(ones, weights_ref[g, 0])
        for j in range(1, per_row):
            degree += times_transposed(ones, weights_ref[g, j])
        inv = lax.rsqrt(degree[:1])
        inv_ref[g : g + 1, :] = inv
        x = signal_ref[:, g * width : (g + 1) * width].astype(F32)
        scaled_ref[g] = (x * inv).astype(BF16)
    pack(send_ref, scaled_ref, packs)


def gather_sources(scaled_ref, received, source):
    blocks = scaled_ref.shape[0]
    source[:blocks] = scaled_ref[...]
    for way, ref in enumerate(received):
        slots = ref.shape[0]
        source[blocks + way * slots : blocks + (way + 1) * slots] = ref[...]


def block_product(g, col_ref, weights_ref, source):
    per_row = weights_ref.shape[1]
    picked = jnp.concatenate([source[col_ref[g, j]] for j in range(per_row)], axis=1)
    edges = jnp.concatenate([weights_ref[g, j] for j in range(per_row)], axis=1)
    return times_transposed(picked, edges)


def first_product(scaled_ref, r0, r1, r2, r3, weights_ref, inv_ref, col_ref, send_ref, term_ref, next_ref, *rest):
    *packs, source = rest
    gather_sources(scaled_ref, (r0, r1, r2, r3), source)
    for g in range(weights_ref.shape[0]):
        inv = inv_ref[g : g + 1, :]
        term = (-inv * block_product(g, col_ref, weights_ref, source)).astype(BF16)
        term_ref[g] = term
        next_ref[g] = (inv * term.astype(F32)).astype(BF16)
    pack(send_ref, next_ref, packs)


def second_product(next_ref, r0, r1, r2, r3, weights_ref, inv_ref, col_ref, coef_ref, signal_ref, term_ref, mixed_ref, source):
    width = weights_ref.shape[2]
    gather_sources(next_ref, (r0, r1, r2, r3), source)
    for g in range(weights_ref.shape[0]):
        inv = inv_ref[g : g + 1, :]
        total = block_product(g, col_ref, weights_ref, source)
        x = signal_ref[:, g * width : (g + 1) * width].astype(F32)
        two = (-2.0 * inv * total - x).astype(BF16).astype(F32)
        one = term_ref[g].astype(F32)
        mixed_ref[g] = (coef_ref[0] * x + coef_ref[1] * one + coef_ref[2] * two).astype(BF16)


def temporal(t_loc, field_ref, kernel_ref, out_ref, whole):
    owners, rows, width = field_ref.shape
    mix = kernel_ref[...].astype(BF16)
    for p in range(rows // t_loc):
        part = slice(p * t_loc, (p + 1) * t_loc)
        for i in range(owners):
            whole[i * t_loc : (i + 1) * t_loc, p * width : (p + 1) * width] = field_ref[i, part]
    step = 2 * width
    for c in range(whole.shape[1] // step):
        out = jnp.dot(mix, whole[:, c * step : (c + 1) * step], preferred_element_type=F32).astype(BF16)
        for q in range(step // width):
            p = c * (step // width) + q
            for i in range(owners):
                out_ref[i, p * t_loc : (p + 1) * t_loc] = out[i * t_loc : (i + 1) * t_loc, q * width : (q + 1) * width]


def unblock(field_ref, out_ref):
    blocks, _, width = field_ref.shape
    for g in range(blocks):
        out_ref[:, g * width : (g + 1) * width] = field_ref[g]


def halo(packs):
    count = lax.axis_size("dom")
    return [
        lax.ppermute(block, "dom", [(i, (i - distance) % count) for i in range(count)])
        for block, distance in zip(packs, OFFSETS)
    ]


def exchange(field):
    return lax.all_to_all(field, "tm", split_axis=0, concat_axis=0, tiled=True)


def body(signal, weights, send_list, col_ref, kernel, cheb_coef):
    probes, t_loc, n_loc = signal.shape
    blocks, per_row, width, _ = weights.shape
    rows = probes * t_loc
    slots = send_list.shape[2]
    owners = lax.axis_size("tm")
    time = kernel.shape[1]
    xs = signal.reshape(rows, n_loc)
    field = array(blocks, rows, width)
    packed = [array(slots, rows, width)] * len(OFFSETS)
    source = pltpu.VMEM((blocks + len(OFFSETS) * slots, rows, width), BF16)
    work = 2 * rows * per_row * n_loc * width

    mix = lax.all_gather(kernel.astype(F32), "tm", axis=0, tiled=True)
    scaled, inv, *packs = call(
        first_scale, [field, array(blocks, width, dtype=F32), *packed], (xs, weights, send_list), flops=work // 16
    )
    term, nxt, *packs = call(
        first_product,
        [field, field, *packed],
        (scaled, *halo(packs), weights, inv, col_ref, send_list),
        [source],
        flops=work,
    )
    (mixed,) = call(
        second_product, [field], (nxt, *halo(packs), weights, inv, col_ref, cheb_coef, xs, term), [source], flops=work
    )
    (filtered,) = call(
        functools.partial(temporal, t_loc),
        [array(owners, rows, width)],
        (exchange(mixed), mix),
        [pltpu.VMEM((time, probes * width), BF16)],
        flops=2 * time * time * probes * width,
    )
    (out,) = call(unblock, [array(rows, n_loc)], (exchange(filtered),))
    return out.reshape(probes, t_loc, n_loc)


def solution(mesh):
    in_specs = (
        P(None, "tm", "dom"),
        P("dom", None, None, None),
        P("dom", None, None),
        P("dom", None),
        P("tm", None),
        P(),
    )
    out_specs = P(None, "tm", "dom")
    return jax.shard_map(body, mesh=mesh, in_specs=in_specs, out_specs=out_specs, check_vma=False)
```

```python
import functools

import jax
import jax.numpy as jnp
from jax import lax
from jax.experimental import pallas as pl
from jax.experimental.pallas import tpu as pltpu
from jax.sharding import PartitionSpec as P

REACH = 2
OFFSETS = tuple(range(-REACH, 0)) + tuple(range(1, REACH + 1))
F32, BF16 = jnp.float32, jnp.bfloat16
LIMIT = 24 * 2**20


def whole(a):
    return pl.BlockSpec(a.shape, lambda i: (0,) * len(a.shape))


def half(a, part):
    return pl.BlockSpec((a.shape[0] // 2, a.shape[1]), lambda i: (part, 0))


SMEM = pl.BlockSpec(memory_space=pltpu.SMEM)


def call(kernel, outs, ins, scratch=(), flops=0, in_specs=None, out_specs=None, aliases=None):
    size = sum(a.size * a.dtype.itemsize for a in (*ins, *outs))
    specs = [SMEM if a.dtype == jnp.int32 or a.size < 8 else whole(a) for a in ins]
    for i, spec in (in_specs or {}).items():
        specs[i] = spec
    results = [whole(a) for a in outs]
    for i, spec in (out_specs or {}).items():
        results[i] = spec
    return pl.pallas_call(
        kernel,
        grid=(1,),
        out_shape=outs,
        in_specs=specs,
        out_specs=results,
        scratch_shapes=list(scratch),
        compiler_params=pltpu.CompilerParams(vmem_limit_bytes=LIMIT),
        cost_estimate=pl.CostEstimate(flops=flops, bytes_accessed=size, transcendentals=0),
        input_output_aliases=aliases or {},
    )(*ins)


def array(*shape, dtype=BF16):
    return jax.ShapeDtypeStruct(shape, dtype)


def times_transposed(a, b):
    return lax.dot_general(a, b, (((1,), (1,)), ((), ())), preferred_element_type=F32)


def block_of(ref, g, width):
    if len(ref.shape) == 3:
        return ref[g]
    start = g * width
    return ref[:, pl.ds(start if isinstance(g, int) else pl.multiple_of(start, width), width)]


def scaled_block(ref, inv_ref, g, width):
    return (block_of(ref, g, width).astype(F32) * inv_ref[pl.ds(g, 1), :]).astype(BF16)


def pack(send_ref, field_ref, inv_ref, packs):
    width = inv_ref.shape[1]
    for way, out in enumerate(packs):
        for slot in range(out.shape[0]):
            out[slot] = scaled_block(field_ref, inv_ref, send_ref[0, way, slot], width)


def lay_out(signal_ref, kernel_ref, out_ref):
    owners, _, width = out_ref.shape
    rows, t_loc = signal_ref.shape[0], kernel_ref.shape[0]
    for i in range(owners):
        out_ref[i, :rows] = signal_ref[:, i * width : (i + 1) * width]
        for q in range(kernel_ref.shape[1] // width):
            out_ref[i, rows + q * t_loc : rows + (q + 1) * t_loc] = kernel_ref[:, q * width : (q + 1) * width]


def first_scale(signal_ref, weights_ref, send_ref, inv_ref, *packs):
    blocks, per_row, width, _ = weights_ref.shape
    ones = jnp.ones((16, width), BF16)
    for g in range(blocks):
        degree = times_transposed(ones, weights_ref[g, 0])
        for j in range(1, per_row):
            degree += times_transposed(ones, weights_ref[g, j])
        inv_ref[g : g + 1, :] = lax.rsqrt(degree[:1])
    pack(send_ref, signal_ref, inv_ref, packs)


def scale(field_ref, inv_ref, send_ref, *packs):
    pack(send_ref, field_ref, inv_ref, packs)


def gather_sources(field_ref, inv_ref, received, source):
    blocks, width = inv_ref.shape
    for g in range(blocks):
        source[g] = scaled_block(field_ref, inv_ref, g, width)
    for way, ref in enumerate(received):
        slots = ref.shape[0]
        source[blocks + way * slots : blocks + (way + 1) * slots] = ref[...]


def block_product(g, col_ref, weights_ref, source):
    per_row = weights_ref.shape[1]
    picked = jnp.concatenate([source[col_ref[g, j]] for j in range(per_row)], axis=1)
    edges = jnp.concatenate([weights_ref[g, j] for j in range(per_row)], axis=1)
    return times_transposed(picked, edges)


def first_product(field_ref, r0, r1, r2, r3, weights_ref, inv_ref, col_ref, send_ref, term_ref, *rest):
    *packs, source = rest
    gather_sources(field_ref, inv_ref, (r0, r1, r2, r3), source)
    for g in range(weights_ref.shape[0]):
        total = block_product(g, col_ref, weights_ref, source)
        term_ref[g] = (-inv_ref[g : g + 1, :] * total).astype(BF16)
    pack(send_ref, term_ref, inv_ref, packs)


def second_product(field_ref, r0, r1, r2, r3, weights_ref, inv_ref, col_ref, coef_ref, term_ref, out_ref, source):
    width = weights_ref.shape[2]
    gather_sources(term_ref, inv_ref, (r0, r1, r2, r3), source)
    for g in range(weights_ref.shape[0]):
        total = block_product(g, col_ref, weights_ref, source)
        x = block_of(field_ref, g, width).astype(F32)
        two = (-2.0 * inv_ref[g : g + 1, :] * total - x).astype(BF16).astype(F32)
        one = term_ref[g].astype(F32)
        mixed = (coef_ref[0] * x + coef_ref[1] * one + coef_ref[2] * two).astype(BF16)
        if len(out_ref.shape) == 3:
            out_ref[g] = mixed
        else:
            out_ref[:, g * width : (g + 1) * width] = mixed


def mix_times(t_loc, rows, mix, field_ref, out_ref, columns):
    owners, _, width = field_ref.shape
    for p in range(rows // t_loc):
        part = slice(p * t_loc, (p + 1) * t_loc)
        for i in range(owners):
            columns[i * t_loc : (i + 1) * t_loc, p * width : (p + 1) * width] = field_ref[i, part]
    step = 2 * width
    for c in range(columns.shape[1] // step):
        out = jnp.dot(mix, columns[:, c * step : (c + 1) * step], preferred_element_type=F32).astype(BF16)
        for q in range(step // width):
            p = c * (step // width) + q
            for i in range(owners):
                out_ref[i, p * t_loc : (p + 1) * t_loc] = out[i * t_loc : (i + 1) * t_loc, q * width : (q + 1) * width]


def first_temporal(t_loc, field_ref, out_ref, mix_ref, columns):
    owners, _, width = field_ref.shape
    rows = out_ref.shape[1]
    for i in range(owners):
        for q in range(mix_ref.shape[1] // width):
            mix_ref[i * t_loc : (i + 1) * t_loc, q * width : (q + 1) * width] = field_ref[
                i, rows + q * t_loc : rows + (q + 1) * t_loc
            ]
    mix_times(t_loc, rows, mix_ref[...], field_ref, out_ref, columns)


def second_temporal(t_loc, field_ref, mix_ref, out_ref, columns):
    mix_times(t_loc, out_ref.shape[1], mix_ref[...], field_ref, out_ref, columns)


def unblock(_, field_ref, out_ref):
    blocks, _, width = field_ref.shape
    for g in range(blocks):
        out_ref[:, g * width : (g + 1) * width] = field_ref[g]


def halo(packs):
    count = lax.axis_size("dom")
    return [
        lax.ppermute(block, "dom", [(i, (i - distance) % count) for i in range(count)])
        for block, distance in zip(packs, OFFSETS)
    ]


def exchange(field):
    return lax.all_to_all(field, "tm", split_axis=0, concat_axis=0, tiled=True)


def body(signal, weights, send_list, col_ref, kernel, cheb_coef):
    probes, t_loc, n_loc = signal.shape
    blocks, per_row, width, _ = weights.shape
    rows = probes * t_loc // 2
    slots = send_list.shape[2]
    owners = lax.axis_size("tm")
    time = kernel.shape[1]
    xs = signal.reshape(2 * rows, n_loc)
    front, back = half(xs, 0), half(xs, 1)
    field = array(blocks, rows, width)
    packed = [array(slots, rows, width)] * len(OFFSETS)
    source = pltpu.VMEM((blocks + len(OFFSETS) * slots, rows, width), BF16)
    columns = pltpu.VMEM((time, rows // t_loc * width), BF16)
    work = 2 * rows * per_row * n_loc * width
    mixing = 2 * time * time * rows // t_loc * width
    shared = (weights,)

    def one(x, packs, inv, spec):
        term, *packs = call(
            first_product,
            [field, *packed],
            (x, *halo(packs), *shared, inv, col_ref, send_list),
            [source],
            flops=work,
            in_specs=spec,
        )
        return term, packs

    def two(x, packs, inv, term, out, spec, out_spec):
        return call(
            second_product,
            [out],
            (x, *halo(packs), *shared, inv, col_ref, cheb_coef, term),
            [source],
            flops=work,
            in_specs=spec,
            out_specs=out_spec,
        )[0]

    chunk = rows + time * t_loc // width
    (laid,) = call(lay_out, [array(owners, chunk, width)], (xs, kernel), in_specs={0: front})
    arrived = exchange(laid)
    inv, *packs = call(
        first_scale,
        [array(blocks, width, dtype=F32), *packed],
        (xs, weights, send_list),
        flops=work // 8,
        in_specs={0: back},
    )
    term, packs = one(xs, packs, inv, {0: back})
    early, mix = call(
        functools.partial(first_temporal, t_loc), [field, array(time, time)], (arrived,), [columns], flops=mixing
    )
    early, *packs = lax.optimization_barrier((early, *packs))
    early = exchange(early)
    late = two(xs, packs, inv, term, field, {0: back}, {})
    late, early = lax.optimization_barrier((late, early))
    late = exchange(late)
    packs = call(scale, packed, (early, inv, send_list))
    term, packs = one(early, packs, inv, {})
    (late,) = call(functools.partial(second_temporal, t_loc), [field], (late, mix), [columns], flops=mixing)
    late, *packs = lax.optimization_barrier((late, *packs))
    late = exchange(late)
    out = array(2 * rows, n_loc)
    done = two(early, packs, inv, term, out, {}, {0: half(out, 0)})
    (done,) = call(
        unblock,
        [out],
        (done, late),
        in_specs={0: pl.BlockSpec(memory_space=pl.ANY)},
        out_specs={0: half(out, 1)},
        aliases={0: 0},
    )
    return done.reshape(probes, t_loc, n_loc)


def solution(mesh):
    in_specs = (
        P(None, "tm", "dom"),
        P("dom", None, None, None),
        P("dom", None, None),
        P("dom", None),
        P("tm", None),
        P(),
    )
    out_specs = P(None, "tm", "dom")
    return jax.shard_map(body, mesh=mesh, in_specs=in_specs, out_specs=out_specs, check_vma=False)
```

```python
import functools

import jax
import jax.numpy as jnp
from jax import lax
from jax.experimental import pallas as pl
from jax.experimental.pallas import tpu as pltpu
from jax.sharding import PartitionSpec as P

REACH = 2
OFFSETS = tuple(range(-REACH, 0)) + tuple(range(1, REACH + 1))
F32, BF16 = jnp.float32, jnp.bfloat16
LIMIT = 24 * 2**20
SMEM = pl.BlockSpec(memory_space=pltpu.SMEM)
VMEM = pl.BlockSpec(memory_space=pltpu.VMEM)
HBM = pl.BlockSpec(memory_space=pltpu.HBM)
ANY = pl.BlockSpec(memory_space=pl.ANY)
DMA = pltpu.SemaphoreType.DMA


def call(kernel, outs, ins, scratch, flops=0, aliases=None):
    arrays, specs = zip(*ins)
    shapes, results = zip(*outs)
    size = sum(a.size * a.dtype.itemsize for a in (*arrays, *shapes))
    arrays = [pltpu.with_memory_space_constraint(a, pltpu.HBM) if spec is HBM else a for a, spec in ins]
    shapes = [pltpu.HBM(a.shape, a.dtype) if spec is HBM else a for a, spec in outs]
    return pl.pallas_call(
        kernel,
        out_shape=shapes,
        in_specs=specs,
        out_specs=results,
        scratch_shapes=scratch,
        compiler_params=pltpu.CompilerParams(vmem_limit_bytes=LIMIT),
        cost_estimate=pl.CostEstimate(flops=flops, bytes_accessed=size, transcendentals=0),
        input_output_aliases=aliases or {},
    )(*arrays)


def array(*shape, dtype=BF16):
    return jax.ShapeDtypeStruct(shape, dtype)


def start(source, target, sem):
    copy = pltpu.make_async_copy(source, target, sem)
    copy.start()
    return copy


def wait(copies):
    for copy in copies:
        copy.wait()


def times_transposed(a, b):
    return lax.dot_general(a, b, (((1,), (1,)), ((), ())), preferred_element_type=F32)


def block_of(ref, g, width):
    if len(ref.shape) == 3:
        return ref[g]
    at = g * width
    return ref[:, pl.ds(at if isinstance(g, int) else pl.multiple_of(at, width), width)]


def scaled_block(ref, inv_ref, g, width):
    return (block_of(ref, g, width).astype(F32) * inv_ref[pl.ds(g, 1), :]).astype(BF16)


def pack(send_ref, field_ref, inv_ref, packs, held, sems):
    width = inv_ref.shape[1]
    copies = []
    for way, out in enumerate(packs):
        for slot in range(out.shape[0]):
            held[way, slot] = scaled_block(field_ref, inv_ref, send_ref[0, way, slot], width)
        copies.append(start(held.at[way], out, sems.at[way]))
    return copies


def lay_out(signal_ref, kernel_ref, out_ref, held, mix, in_sems, out_sems, mix_sem):
    owners, chunk, width = out_ref.shape
    t_loc, time = kernel_ref.shape
    rows = chunk - time * t_loc // width
    mixing = start(kernel_ref, mix, mix_sem)
    loads = [
        start(signal_ref.at[:rows, i * width : (i + 1) * width], held.at[i, :rows], in_sems.at[i])
        for i in range(owners)
    ]
    mixing.wait()
    copies = []
    for i in range(owners):
        for q in range(time // width):
            held[i, rows + q * t_loc : rows + (q + 1) * t_loc] = mix[:, q * width : (q + 1) * width]
        loads[i].wait()
        copies.append(start(held.at[i], out_ref.at[i], out_sems.at[i]))
    wait(copies)


def first_scale(signal_ref, weights_ref, send_ref, coef_ref, inv_ref, *rest):
    *packs, field, held, sems, load_sem = rest
    blocks, per_row, width, _ = weights_ref.shape
    rows = field.shape[0]
    load = start(signal_ref.at[rows:], field, load_sem)
    ones = jnp.ones((16, width), BF16)
    for g in range(blocks):
        degree = times_transposed(ones, weights_ref[g, 0])
        for j in range(1, per_row):
            degree += times_transposed(ones, weights_ref[g, j])
        inv_ref[g : g + 1, :] = lax.rsqrt(degree[:1])
    for term in range(coef_ref.shape[0]):
        inv_ref[blocks + term : blocks + term + 1, :] = jnp.full((1, width), coef_ref[term], F32)
    load.wait()
    wait(pack(send_ref, field, inv_ref, packs, held, sems))


def scale(field_ref, inv_ref, send_ref, *rest):
    *packs, held, sems = rest
    wait(pack(send_ref, field_ref, inv_ref, packs, held, sems))


def gather_sources(blocks, field_ref, inv_ref, received, source):
    width = inv_ref.shape[1]
    for g in range(blocks):
        source[g] = scaled_block(field_ref, inv_ref, g, width)
    for way, ref in enumerate(received):
        slots = ref.shape[0]
        source[blocks + way * slots : blocks + (way + 1) * slots] = ref[...]


def block_product(g, col_ref, weights_ref, source):
    per_row = weights_ref.shape[1]
    picked = jnp.concatenate([source[col_ref[g, j]] for j in range(per_row)], axis=1)
    edges = jnp.concatenate([weights_ref[g, j] for j in range(per_row)], axis=1)
    return times_transposed(picked, edges)


def load_half(field_ref, field, sem):
    return [start(field_ref.at[field.shape[0] :], field, sem)]


def first_product(in_hbm, field_ref, r0, r1, r2, r3, weights_ref, inv_ref, col_ref, send_ref, term_ref, *rest):
    *packs, source, term, held, sems, pack_sems = rest[: len(OFFSETS) + 5]
    if in_hbm:
        field, load_sem = rest[len(OFFSETS) + 5 :]
        wait(load_half(field_ref, field, load_sem))
        field_ref = field
    blocks = weights_ref.shape[0]
    gather_sources(blocks, field_ref, inv_ref, (r0, r1, r2, r3), source)
    copies = []
    for g in range(blocks):
        total = block_product(g, col_ref, weights_ref, source)
        term[g] = (-inv_ref[g : g + 1, :] * total).astype(BF16)
        copies.append(start(term.at[g], term_ref.at[g], sems.at[g]))
    wait(copies + pack(send_ref, term, inv_ref, packs, held, pack_sems))


def second_product(in_hbm, field_ref, r0, r1, r2, r3, weights_ref, inv_ref, col_ref, term_ref, out_ref, *rest):
    source, term, held, sems, term_sem = rest[:5]
    loads = [start(term_ref, term, term_sem)]
    if in_hbm:
        field, load_sem = rest[5:]
        loads += load_half(field_ref, field, load_sem)
        field_ref = field
    wait(loads)
    blocks, _, width, _ = weights_ref.shape
    rows = term.shape[1]
    gather_sources(blocks, term, inv_ref, (r0, r1, r2, r3), source)
    coef = [inv_ref[blocks + i : blocks + i + 1, :] for i in range(3)]
    copies = []
    for g in range(blocks):
        total = block_product(g, col_ref, weights_ref, source)
        x = block_of(field_ref, g, width).astype(F32)
        two = (-2.0 * inv_ref[g : g + 1, :] * total - x).astype(BF16).astype(F32)
        one = term[g].astype(F32)
        held[g] = (coef[0] * x + coef[1] * one + coef[2] * two).astype(BF16)
        if len(out_ref.shape) == 3:
            target = out_ref.at[g]
        else:
            target = out_ref.at[:rows, g * width : (g + 1) * width]
        copies.append(start(held.at[g], target, sems.at[g]))
    wait(copies)


def mix_times(t_loc, mix, field_ref, out_ref, columns, held, sems):
    owners, rows, width = out_ref.shape
    for p in range(rows // t_loc):
        part = slice(p * t_loc, (p + 1) * t_loc)
        for i in range(owners):
            columns[i * t_loc : (i + 1) * t_loc, p * width : (p + 1) * width] = field_ref[i, part]
    step = 2 * width
    pieces = columns.shape[1] // step
    depth = rows // pieces
    copies = []
    for c in range(pieces):
        out = jnp.dot(mix, columns[:, c * step : (c + 1) * step], preferred_element_type=F32).astype(BF16)
        for q in range(step // width):
            at = c * depth + q * t_loc
            for i in range(owners):
                held[i, at : at + t_loc] = out[i * t_loc : (i + 1) * t_loc, q * width : (q + 1) * width]
        part = slice(c * depth, (c + 1) * depth)
        copies.append(start(held.at[:, part], out_ref.at[:, part], sems.at[c]))
    return copies


def first_temporal(t_loc, field_ref, out_ref, mix_ref, columns, held, mix, sems, mix_sem):
    owners, rows, width = out_ref.shape
    for i in range(owners):
        for q in range(mix.shape[1] // width):
            mix[i * t_loc : (i + 1) * t_loc, q * width : (q + 1) * width] = field_ref[
                i, rows + q * t_loc : rows + (q + 1) * t_loc
            ]
    keep = start(mix, mix_ref, mix_sem)
    wait(mix_times(t_loc, mix[...], field_ref, out_ref, columns, held, sems) + [keep])


def second_temporal(t_loc, field_ref, mix_ref, out_ref, columns, held, mix, sems, mix_sem):
    start(mix_ref, mix, mix_sem).wait()
    wait(mix_times(t_loc, mix[...], field_ref, out_ref, columns, held, sems))


def unblock(_, field_ref, out_ref, sems):
    blocks, rows, width = field_ref.shape
    wait(
        [
            start(field_ref.at[g], out_ref.at[rows:, g * width : (g + 1) * width], sems.at[g])
            for g in range(blocks)
        ]
    )


def take(block, way):
    count = lax.axis_size("dom")
    return lax.ppermute(block, "dom", [(i, (i - OFFSETS[way]) % count) for i in range(count)])


def exchange(field):
    return lax.all_to_all(field, "tm", split_axis=0, concat_axis=0, tiled=True)


def body(signal, weights, send_list, col_ref, kernel, cheb_coef):
    probes, t_loc, n_loc = signal.shape
    blocks, per_row, width, _ = weights.shape
    rows = probes * t_loc // 2
    slots = send_list.shape[2]
    owners = lax.axis_size("tm")
    time = kernel.shape[1]
    ways = len(OFFSETS)
    pieces = rows // t_loc // 2
    xs = signal.reshape(2 * rows, n_loc)
    field = array(blocks, rows, width)
    packed = [(array(slots, rows, width), HBM)] * ways
    vm = pltpu.VMEM
    source = vm((blocks + ways * slots, rows, width), BF16)
    whole = vm((blocks, rows, width), BF16)
    held = vm((ways, slots, rows, width), BF16)
    second_half = [vm((rows, n_loc), BF16), DMA]
    mixer = [vm((time, rows // t_loc * width), BF16), whole, vm((time, time), BF16), DMA((pieces,)), DMA]
    work = 2 * rows * per_row * n_loc * width
    mixing = 2 * time * time * rows // t_loc * width
    barrier = lax.optimization_barrier

    def one(x, received, inv, in_hbm):
        term, *packs = call(
            functools.partial(first_product, in_hbm),
            [(field, HBM), *packed],
            [
                (x, HBM if in_hbm else VMEM),
                *((r, VMEM) for r in received),
                (weights, VMEM),
                (inv, VMEM),
                (col_ref, SMEM),
                (send_list, SMEM),
            ],
            [source, whole, held, DMA((blocks,)), DMA((ways,))] + (second_half if in_hbm else []),
            flops=work,
        )
        return term, packs

    def two(x, received, inv, term, out, in_hbm):
        return call(
            functools.partial(second_product, in_hbm),
            [(out, HBM)],
            [
                (x, HBM if in_hbm else VMEM),
                *((r, VMEM) for r in received),
                (weights, VMEM),
                (inv, VMEM),
                (col_ref, SMEM),
                (term, HBM),
            ],
            [source, whole, whole, DMA((blocks,)), DMA] + (second_half if in_hbm else []),
            flops=work,
        )[0]

    chunk = rows + time * t_loc // width
    (laid,) = call(
        lay_out,
        [(array(owners, chunk, width), HBM)],
        [(xs, HBM), (kernel, HBM)],
        [vm((owners, chunk, width), BF16), vm(kernel.shape, BF16), DMA((owners,)), DMA((owners,)), DMA],
    )
    arrived = exchange(laid)
    inv, *packs = call(
        first_scale,
        [(array(blocks + 8, width, dtype=F32), VMEM), *packed],
        [(xs, HBM), (weights, VMEM), (send_list, SMEM), (cheb_coef, SMEM)],
        [vm((rows, n_loc), BF16), held, DMA((ways,)), DMA],
        flops=work // 8,
    )
    received = [take(block, way) for way, block in enumerate(packs)]
    term, packs = one(xs, received, inv, True)

    received = [take(packs[way], way) for way in range(ways // 2)]
    early, mix = call(
        functools.partial(first_temporal, t_loc),
        [(field, HBM), (array(time, time), HBM)],
        [(arrived, VMEM)],
        mixer,
        flops=mixing,
    )
    early, *rest = barrier((early, *packs[ways // 2 :]))
    early = exchange(early)
    received += [take(block, ways // 2 + i) for i, block in enumerate(rest)]

    packs = call(scale, packed, [(early, VMEM), (inv, VMEM), (send_list, SMEM)], [held, DMA((ways,))])
    term, *packs = barrier((term, *packs))
    later = [take(packs[way], way) for way in range(ways // 2)]
    late = two(xs, received, inv, term, field, True)
    late, *rest = barrier((late, *packs[ways // 2 :]))
    late = exchange(late)
    received = later + [take(block, ways // 2 + i) for i, block in enumerate(rest)]
    term, packs = one(early, received, inv, False)

    received = [take(packs[way], way) for way in range(ways // 2)]
    (late,) = call(
        functools.partial(second_temporal, t_loc), [(field, HBM)], [(late, VMEM), (mix, HBM)], mixer, flops=mixing
    )
    late, *rest = barrier((late, *packs[ways // 2 :]))
    late = exchange(late)
    received += [take(block, ways // 2 + i) for i, block in enumerate(rest)]
    out = array(2 * rows, n_loc)
    done = two(early, received, inv, term, out, False)
    (done,) = call(unblock, [(out, HBM)], [(done, HBM), (late, ANY)], [DMA((blocks,))], aliases={0: 0})
    return done.reshape(probes, t_loc, n_loc)


def solution(mesh):
    in_specs = (
        P(None, "tm", "dom"),
        P("dom", None, None, None),
        P("dom", None, None),
        P("dom", None),
        P("tm", None),
        P(),
    )
    out_specs = P(None, "tm", "dom")
    return jax.shard_map(body, mesh=mesh, in_specs=in_specs, out_specs=out_specs, check_vma=False)
```

```python
import functools

import jax
import jax.numpy as jnp
from jax import lax
from jax.experimental import pallas as pl
from jax.experimental.pallas import tpu as pltpu
from jax.sharding import PartitionSpec as P

REACH = 2
OFFSETS = tuple(range(-REACH, 0)) + tuple(range(1, REACH + 1))
F32, BF16 = jnp.float32, jnp.bfloat16
LIMIT = 24 * 2**20
SMEM = pl.BlockSpec(memory_space=pltpu.SMEM)
VMEM = pl.BlockSpec(memory_space=pltpu.VMEM)
HBM = pl.BlockSpec(memory_space=pltpu.HBM)
DMA = pltpu.SemaphoreType.DMA


def call(kernel, outs, ins, scratch, flops=0, aliases=None):
    arrays, specs = zip(*ins)
    shapes, results = zip(*outs)
    size = sum(a.size * a.dtype.itemsize for a in (*arrays, *shapes))
    arrays = [pltpu.with_memory_space_constraint(a, pltpu.HBM) if spec is HBM else a for a, spec in ins]
    shapes = [pltpu.HBM(a.shape, a.dtype) if spec is HBM else a for a, spec in outs]
    return pl.pallas_call(
        kernel,
        out_shape=shapes,
        in_specs=specs,
        out_specs=results,
        scratch_shapes=scratch,
        compiler_params=pltpu.CompilerParams(vmem_limit_bytes=LIMIT),
        cost_estimate=pl.CostEstimate(flops=flops, bytes_accessed=size, transcendentals=0),
        input_output_aliases=aliases or {},
    )(*arrays)


def array(*shape, dtype=BF16):
    return jax.ShapeDtypeStruct(shape, dtype)


def start(source, target, sem):
    copy = pltpu.make_async_copy(source, target, sem)
    copy.start()
    return copy


def wait(copies):
    for copy in copies:
        copy.wait()


def times_transposed(a, b):
    return lax.dot_general(a, b, (((1,), (1,)), ((), ())), preferred_element_type=F32)


def block_of(ref, g, width):
    if len(ref.shape) == 3:
        return ref[g]
    at = g * width
    return ref[:, pl.ds(at if isinstance(g, int) else pl.multiple_of(at, width), width)]


def scaled_block(ref, inv_ref, g, width):
    return (block_of(ref, g, width).astype(F32) * inv_ref[pl.ds(g, 1), :]).astype(BF16)


def pack(send_ref, field_ref, inv_ref, packs, held, sems):
    width = inv_ref.shape[1]
    copies = []
    for way, out in enumerate(packs):
        for slot in range(out.shape[0]):
            held[way, slot] = scaled_block(field_ref, inv_ref, send_ref[0, way, slot], width)
        copies.append(start(held.at[way], out, sems.at[way]))
    return copies


def lay_out(signal_ref, kernel_ref, out_ref, held, mix, in_sems, out_sems, mix_sem):
    owners, chunk, width = out_ref.shape
    t_loc, time = kernel_ref.shape
    rows = chunk - time * t_loc // width
    mixing = start(kernel_ref, mix, mix_sem)
    loads = [
        start(signal_ref.at[:rows, i * width : (i + 1) * width], held.at[i, :rows], in_sems.at[i])
        for i in range(owners)
    ]
    mixing.wait()
    copies = []
    for i in range(owners):
        for q in range(time // width):
            held[i, rows + q * t_loc : rows + (q + 1) * t_loc] = mix[:, q * width : (q + 1) * width]
        loads[i].wait()
        copies.append(start(held.at[i], out_ref.at[i], out_sems.at[i]))
    wait(copies)


def first_scale(signal_ref, weights_ref, send_ref, coef_ref, inv_ref, *rest):
    *packs, field, held, sems, load_sem = rest
    blocks, per_row, width, _ = weights_ref.shape
    rows = field.shape[0]
    load = start(signal_ref.at[rows:], field, load_sem)
    ones = jnp.ones((16, width), BF16)
    for g in range(blocks):
        degree = times_transposed(ones, weights_ref[g, 0])
        for j in range(1, per_row):
            degree += times_transposed(ones, weights_ref[g, j])
        inv_ref[g : g + 1, :] = lax.rsqrt(degree[:1])
    for term in range(coef_ref.shape[0]):
        inv_ref[blocks + term : blocks + term + 1, :] = jnp.full((1, width), coef_ref[term], F32)
    load.wait()
    wait(pack(send_ref, field, inv_ref, packs, held, sems))


def scale(field_ref, inv_ref, send_ref, *rest):
    *packs, held, sems = rest
    wait(pack(send_ref, field_ref, inv_ref, packs, held, sems))


def gather_sources(blocks, field_ref, inv_ref, received, source):
    width = inv_ref.shape[1]
    for g in range(blocks):
        source[g] = scaled_block(field_ref, inv_ref, g, width)
    for way, ref in enumerate(received):
        slots = ref.shape[0]
        source[blocks + way * slots : blocks + (way + 1) * slots] = ref[...]


def block_product(g, col_ref, weights_ref, source):
    per_row = weights_ref.shape[1]
    picked = jnp.concatenate([source[col_ref[g, j]] for j in range(per_row)], axis=1)
    edges = jnp.concatenate([weights_ref[g, j] for j in range(per_row)], axis=1)
    return times_transposed(picked, edges)


def load_half(field_ref, field, sem):
    return [start(field_ref.at[field.shape[0] :], field, sem)]


def first_product(in_hbm, field_ref, r0, r1, r2, r3, weights_ref, inv_ref, col_ref, send_ref, term_ref, *rest):
    *packs, source, term, held, sems, pack_sems = rest[: len(OFFSETS) + 5]
    if in_hbm:
        field, load_sem = rest[len(OFFSETS) + 5 :]
        wait(load_half(field_ref, field, load_sem))
        field_ref = field
    blocks = weights_ref.shape[0]
    gather_sources(blocks, field_ref, inv_ref, (r0, r1, r2, r3), source)
    copies = []
    for g in range(blocks):
        total = block_product(g, col_ref, weights_ref, source)
        term[g] = (-inv_ref[g : g + 1, :] * total).astype(BF16)
        copies.append(start(term.at[g], term_ref.at[g], sems.at[g]))
    wait(copies + pack(send_ref, term, inv_ref, packs, held, pack_sems))


def second_product(in_hbm, field_ref, r0, r1, r2, r3, weights_ref, inv_ref, col_ref, term_ref, out_ref, *rest):
    source, term, held, sems, term_sem = rest[:5]
    loads = [start(term_ref, term, term_sem)]
    if in_hbm:
        field, load_sem = rest[5:]
        loads += load_half(field_ref, field, load_sem)
        field_ref = field
    wait(loads)
    blocks, _, width, _ = weights_ref.shape
    rows = term.shape[1]
    gather_sources(blocks, term, inv_ref, (r0, r1, r2, r3), source)
    coef = [inv_ref[blocks + i : blocks + i + 1, :] for i in range(3)]
    copies = []
    for g in range(blocks):
        total = block_product(g, col_ref, weights_ref, source)
        x = block_of(field_ref, g, width).astype(F32)
        two = (-2.0 * inv_ref[g : g + 1, :] * total - x).astype(BF16).astype(F32)
        one = term[g].astype(F32)
        held[g] = (coef[0] * x + coef[1] * one + coef[2] * two).astype(BF16)
        if len(out_ref.shape) == 3:
            target = out_ref.at[g]
        else:
            target = out_ref.at[:rows, g * width : (g + 1) * width]
        copies.append(start(held.at[g], target, sems.at[g]))
    wait(copies)


def mix_times(t_loc, mix, field_ref, out_ref, columns, held, sems):
    owners, rows, width = out_ref.shape
    for p in range(rows // t_loc):
        part = slice(p * t_loc, (p + 1) * t_loc)
        for i in range(owners):
            columns[i * t_loc : (i + 1) * t_loc, p * width : (p + 1) * width] = field_ref[i, part]
    step = 2 * width
    pieces = columns.shape[1] // step
    depth = rows // pieces
    copies = []
    for c in range(pieces):
        out = jnp.dot(mix, columns[:, c * step : (c + 1) * step], preferred_element_type=F32).astype(BF16)
        for q in range(step // width):
            at = c * depth + q * t_loc
            for i in range(owners):
                held[i, at : at + t_loc] = out[i * t_loc : (i + 1) * t_loc, q * width : (q + 1) * width]
        part = slice(c * depth, (c + 1) * depth)
        copies.append(start(held.at[:, part], out_ref.at[:, part], sems.at[c]))
    return copies


def first_temporal(t_loc, field_ref, out_ref, mix_ref, columns, held, mix, sems, mix_sem):
    owners, rows, width = out_ref.shape
    for i in range(owners):
        for q in range(mix.shape[1] // width):
            mix[i * t_loc : (i + 1) * t_loc, q * width : (q + 1) * width] = field_ref[
                i, rows + q * t_loc : rows + (q + 1) * t_loc
            ]
    keep = start(mix, mix_ref, mix_sem)
    wait(mix_times(t_loc, mix[...], field_ref, out_ref, columns, held, sems) + [keep])


def second_temporal(t_loc, field_ref, mix_ref, out_ref, columns, held, mix, sems, mix_sem):
    start(mix_ref, mix, mix_sem).wait()
    wait(mix_times(t_loc, mix[...], field_ref, out_ref, columns, held, sems))


def unblock(_, field_ref, out_ref, sems):
    blocks, rows, width = field_ref.shape
    wait(
        [
            start(field_ref.at[g], out_ref.at[rows:, g * width : (g + 1) * width], sems.at[g])
            for g in range(blocks)
        ]
    )


def take(block, way):
    count = lax.axis_size("dom")
    return lax.ppermute(block, "dom", [(i, (i - OFFSETS[way]) % count) for i in range(count)])


def exchange(field):
    return lax.all_to_all(field, "tm", split_axis=0, concat_axis=0, tiled=True)


def begin(packs, first):
    ways = len(packs)
    ahead = [(first + i) % ways for i in range(ways // 2)]
    behind = [(first + ways // 2 + i) % ways for i in range(ways // 2)]
    got = {way: take(packs[way], way) for way in ahead}

    def finish(field):
        field, *rest = lax.optimization_barrier(
            (field, *(got[way] for way in ahead), *(packs[way] for way in behind))
        )
        field = exchange(field)
        got.update(zip(ahead, rest[: len(ahead)]))
        got.update((way, take(block, way)) for way, block in zip(behind, rest[len(ahead) :]))
        return field, [got[way] for way in range(ways)]

    return finish


def body(signal, weights, send_list, col_ref, kernel, cheb_coef):
    probes, t_loc, n_loc = signal.shape
    blocks, per_row, width, _ = weights.shape
    rows = probes * t_loc // 2
    slots = send_list.shape[2]
    owners = lax.axis_size("tm")
    time = kernel.shape[1]
    ways = len(OFFSETS)
    pieces = rows // t_loc // 2
    xs = signal.reshape(2 * rows, n_loc)
    field = array(blocks, rows, width)
    packed = [(array(slots, rows, width), HBM)] * ways
    vm = pltpu.VMEM
    source = vm((blocks + ways * slots, rows, width), BF16)
    whole = vm((blocks, rows, width), BF16)
    held = vm((ways, slots, rows, width), BF16)
    second_half = [vm((rows, n_loc), BF16), DMA]
    mixer = [vm((time, rows // t_loc * width), BF16), whole, vm((time, time), BF16), DMA((pieces,)), DMA]
    work = 2 * rows * per_row * n_loc * width
    mixing = 2 * time * time * rows // t_loc * width

    def one(x, received, inv, in_hbm):
        term, *packs = call(
            functools.partial(first_product, in_hbm),
            [(field, HBM), *packed],
            [
                (x, HBM if in_hbm else VMEM),
                *((r, VMEM) for r in received),
                (weights, VMEM),
                (inv, VMEM),
                (col_ref, SMEM),
                (send_list, SMEM),
            ],
            [source, whole, held, DMA((blocks,)), DMA((ways,))] + (second_half if in_hbm else []),
            flops=work,
        )
        return term, packs

    def two(x, received, inv, term, out, in_hbm):
        return call(
            functools.partial(second_product, in_hbm),
            [(out, HBM)],
            [
                (x, HBM if in_hbm else VMEM),
                *((r, VMEM) for r in received),
                (weights, VMEM),
                (inv, VMEM),
                (col_ref, SMEM),
                (term, HBM),
            ],
            [source, whole, whole, DMA((blocks,)), DMA] + (second_half if in_hbm else []),
            flops=work,
        )[0]

    chunk = rows + time * t_loc // width
    (laid,) = call(
        lay_out,
        [(array(owners, chunk, width), HBM)],
        [(xs, HBM), (kernel, HBM)],
        [vm((owners, chunk, width), BF16), vm(kernel.shape, BF16), DMA((owners,)), DMA((owners,)), DMA],
    )
    arrived = exchange(laid)
    inv, *packs = call(
        first_scale,
        [(array(blocks + 8, width, dtype=F32), VMEM), *packed],
        [(xs, HBM), (weights, VMEM), (send_list, SMEM), (cheb_coef, SMEM)],
        [vm((rows, n_loc), BF16), held, DMA((ways,)), DMA],
        flops=work // 8,
    )
    received = [take(block, way) for way, block in enumerate(packs)]
    term, packs = one(xs, received, inv, True)

    finish = begin(packs, ways // 2)
    early, mix = call(
        functools.partial(first_temporal, t_loc),
        [(field, HBM), (array(time, time), HBM)],
        [(arrived, VMEM)],
        mixer,
        flops=mixing,
    )
    early, received = finish(early)

    packs = call(scale, packed, [(early, VMEM), (inv, VMEM), (send_list, SMEM)], [held, DMA((ways,))])
    term, *packs = lax.optimization_barrier((term, *packs))
    finish = begin(packs, 0)
    late = two(xs, received, inv, term, field, True)
    late, received = finish(late)
    term, packs = one(early, received, inv, False)

    finish = begin(packs, ways // 2)
    (late,) = call(
        functools.partial(second_temporal, t_loc), [(field, HBM)], [(late, VMEM), (mix, HBM)], mixer, flops=mixing
    )
    late, received = finish(late)
    out = array(2 * rows, n_loc)
    done = two(early, received, inv, term, out, False)
    (done,) = call(unblock, [(out, HBM)], [(done, HBM), (late, VMEM)], [DMA((blocks,))], aliases={0: 0})
    return done.reshape(probes, t_loc, n_loc)


def solution(mesh):
    in_specs = (
        P(None, "tm", "dom"),
        P("dom", None, None, None),
        P("dom", None, None),
        P("dom", None),
        P("tm", None),
        P(),
    )
    out_specs = P(None, "tm", "dom")
    return jax.shard_map(body, mesh=mesh, in_specs=in_specs, out_specs=out_specs, check_vma=False)
```

```python
import functools

import jax
import jax.numpy as jnp
from jax import lax
from jax.experimental import pallas as pl
from jax.experimental.pallas import tpu as pltpu
from jax.sharding import PartitionSpec as P

REACH = 2
OFFSETS = tuple(range(-REACH, 0)) + tuple(range(1, REACH + 1))
F32, BF16 = jnp.float32, jnp.bfloat16
LIMIT = 24 * 2**20
SMEM = pl.BlockSpec(memory_space=pltpu.SMEM)
VMEM = pl.BlockSpec(memory_space=pltpu.VMEM)
HBM = pl.BlockSpec(memory_space=pltpu.HBM)
DMA = pltpu.SemaphoreType.DMA


def call(kernel, outs, ins, scratch, flops=0, aliases=None):
    arrays, specs = zip(*ins)
    shapes, results = zip(*outs)
    size = sum(a.size * a.dtype.itemsize for a in (*arrays, *shapes))
    arrays = [pltpu.with_memory_space_constraint(a, pltpu.HBM) if spec is HBM else a for a, spec in ins]
    shapes = [pltpu.HBM(a.shape, a.dtype) if spec is HBM else a for a, spec in outs]
    return pl.pallas_call(
        kernel,
        out_shape=shapes,
        in_specs=specs,
        out_specs=results,
        scratch_shapes=scratch,
        compiler_params=pltpu.CompilerParams(vmem_limit_bytes=LIMIT),
        cost_estimate=pl.CostEstimate(flops=flops, bytes_accessed=size, transcendentals=0),
        input_output_aliases=aliases or {},
    )(*arrays)


def array(*shape, dtype=BF16):
    return jax.ShapeDtypeStruct(shape, dtype)


def start(source, target, sem):
    copy = pltpu.make_async_copy(source, target, sem)
    copy.start()
    return copy


def wait(copies):
    for copy in copies:
        copy.wait()


def times_transposed(a, b):
    return lax.dot_general(a, b, (((1,), (1,)), ((), ())), preferred_element_type=F32)


def block_of(ref, g, width):
    if len(ref.shape) == 3:
        return ref[g]
    at = g * width
    return ref[:, pl.ds(at if isinstance(g, int) else pl.multiple_of(at, width), width)]


def scaled_block(ref, inv_ref, g, width):
    return (block_of(ref, g, width).astype(F32) * inv_ref[pl.ds(g, 1), :]).astype(BF16)


def partner_ways():
    place = lax.axis_index("dom")
    odd = lax.rem(place, 2)
    upper = lax.div(lax.rem(place, 4), 2)
    return [2 - odd, 1 + odd, 3 * (1 - upper), 3 * upper]


def partners(index, count):
    reach = 1 + index // 2
    down = [(p // reach) % 2 != index % 2 for p in range(count)]
    return [(p, (p - reach if down[p] else p + reach) % count) for p in range(count)]


def pack(send_ref, field_ref, inv_ref, packs, held, sems):
    width = inv_ref.shape[1]
    copies = []
    ways = partner_ways()
    for i in reversed(range(len(packs))):
        out = packs[i]
        way = len(OFFSETS) - 1 - ways[i]
        for slot in range(out.shape[0]):
            held[i, slot] = scaled_block(field_ref, inv_ref, send_ref[0, way, slot], width)
        copies.append(start(held.at[i], out, sems.at[i]))
    return copies


def spread(kernel_ref, out_ref, mix, held, sems, mix_sem):
    owners, _, width = out_ref.shape
    t_loc, time = kernel_ref.shape
    start(kernel_ref, mix, mix_sem).wait()
    for q in range(time // width):
        held[q * t_loc : (q + 1) * t_loc] = mix[:, q * width : (q + 1) * width]
    wait([start(held, out_ref.at[i], sems.at[i]) for i in range(owners)])


def first_scale(signal_ref, weights_ref, send_ref, coef_ref, inv_ref, *rest):
    *packs, field, edges, inv, held, sems, edge_sems, load_sem = rest
    blocks, per_row, width, _ = weights_ref.shape
    loads = [start(weights_ref.at[g], edges.at[g], edge_sems.at[g]) for g in range(blocks)]
    load = start(signal_ref, field, load_sem)
    for term in range(coef_ref.shape[0]):
        inv[blocks + term : blocks + term + 1, :] = jnp.full((1, width), coef_ref[term], F32)
    ones = jnp.ones((16, width), BF16)
    for g in range(blocks):
        loads[g].wait()
        degree = times_transposed(ones, edges[g, 0])
        for j in range(1, per_row):
            degree += times_transposed(ones, edges[g, j])
        inv[g : g + 1, :] = lax.rsqrt(degree[:1])
    load.wait()
    copies = pack(send_ref, field, inv, packs, held, sems)
    wait([start(inv, inv_ref, load_sem), *copies])


def place_received(blocks, received, source):
    for way, ref in zip(partner_ways(), received):
        slots = ref.shape[0]
        for slot in range(slots):
            source[blocks + way * slots + slot] = ref[slot]


def place_own(blocks, field_ref, inv_ref, source):
    for g in range(blocks):
        source[g] = scaled_block(field_ref, inv_ref, g, inv_ref.shape[1])


def block_product(g, col_ref, weights_ref, source):
    per_row = weights_ref.shape[1]
    picked = jnp.concatenate([source[col_ref[g, j]] for j in range(per_row)], axis=1)
    edges = jnp.concatenate([weights_ref[g, j] for j in range(per_row)], axis=1)
    return times_transposed(picked, edges)


def first_product(field_ref, r0, r1, r2, r3, weights_ref, inv_ref, col_ref, send_ref, term_ref, *rest):
    *packs, source, term, held, sems, pack_sems, field, load_sem, inv, inv_sem = rest
    load = start(field_ref, field, load_sem)
    scales = start(inv_ref, inv, inv_sem)
    blocks = weights_ref.shape[0]
    place_received(blocks, (r0, r1, r2, r3), source)
    load.wait()
    scales.wait()
    place_own(blocks, field, inv, source)
    copies = []
    for g in range(blocks):
        total = block_product(g, col_ref, weights_ref, source)
        term[g] = (-inv[g : g + 1, :] * total).astype(BF16)
        copies.append(start(term.at[g], term_ref.at[g], sems.at[g]))
    wait(copies + pack(send_ref, term, inv, packs, held, pack_sems))


def second_product(field_ref, r0, r1, r2, r3, weights_ref, inv_ref, col_ref, term_ref, out_ref, *rest):
    source, term, held, sems, term_sem, field, load_sem, inv, inv_sem = rest
    scales = start(inv_ref, inv, inv_sem)
    first = start(term_ref, term, term_sem)
    load = start(field_ref, field, load_sem)
    blocks, _, width, _ = weights_ref.shape
    place_received(blocks, (r0, r1, r2, r3), source)
    first.wait()
    scales.wait()
    place_own(blocks, term, inv, source)
    coef = [inv[blocks + i : blocks + i + 1, :] for i in range(3)]
    load.wait()
    copies = []
    for g in range(blocks):
        total = block_product(g, col_ref, weights_ref, source)
        x = block_of(field, g, width).astype(F32)
        two = (-2.0 * inv[g : g + 1, :] * total - x).astype(BF16).astype(F32)
        one = term[g].astype(F32)
        held[g] = (coef[0] * x + coef[1] * one + coef[2] * two).astype(BF16)
        copies.append(start(held.at[g], out_ref.at[g], sems.at[g]))
    wait(copies)


def mix_times(t_loc, mix, field_ref, out_ref, columns, held, sems):
    owners, rows, width = out_ref.shape
    for p in range(rows // t_loc):
        part = slice(p * t_loc, (p + 1) * t_loc)
        for i in range(owners):
            columns[i * t_loc : (i + 1) * t_loc, p * width : (p + 1) * width] = field_ref[i, part]
    step = 2 * width
    pieces = columns.shape[1] // step
    depth = rows // pieces
    copies = []
    for c in range(pieces):
        out = jnp.dot(mix, columns[:, c * step : (c + 1) * step], preferred_element_type=F32).astype(BF16)
        for q in range(step // width):
            at = c * depth + q * t_loc
            for i in range(owners):
                held[i, at : at + t_loc] = out[i * t_loc : (i + 1) * t_loc, q * width : (q + 1) * width]
        part = slice(c * depth, (c + 1) * depth)
        copies.append(start(held.at[:, part], out_ref.at[:, part], sems.at[c]))
    return copies


def temporal(t_loc, field_ref, spread_ref, out_ref, columns, held, mix, sems):
    owners = out_ref.shape[0]
    width = out_ref.shape[2]
    for i in range(owners):
        for q in range(mix.shape[1] // width):
            mix[i * t_loc : (i + 1) * t_loc, q * width : (q + 1) * width] = spread_ref[i, q * t_loc : (q + 1) * t_loc]
    wait(mix_times(t_loc, mix[...], field_ref, out_ref, columns, held, sems))


def unblock(field_ref, out_ref, sems):
    blocks, _, width = field_ref.shape
    wait([start(field_ref.at[g], out_ref.at[:, g * width : (g + 1) * width], sems.at[g]) for g in range(blocks)])


def swap(packs):
    count = lax.axis_size("dom")
    return [lax.ppermute(block, "dom", partners(i, count)) for i, block in enumerate(packs)]


def exchange(field):
    return lax.all_to_all(field, "tm", split_axis=0, concat_axis=0, tiled=True)


def body(signal, weights, send_list, col_ref, kernel, cheb_coef):
    probes, t_loc, n_loc = signal.shape
    blocks, per_row, width, _ = weights.shape
    rows = probes * t_loc
    slots = send_list.shape[2]
    owners = lax.axis_size("tm")
    time = kernel.shape[1]
    ways = len(OFFSETS)
    pieces = probes // 2
    xs = signal.reshape(rows, n_loc)
    field = array(blocks, rows, width)
    packed = [(array(slots, rows, width), HBM)] * ways
    vm = pltpu.VMEM
    source = vm((blocks + ways * slots, rows, width), BF16)
    whole = vm((blocks, rows, width), BF16)
    held = vm((ways, slots, rows, width), BF16)
    scales = array(blocks + 8, width, dtype=F32)
    loaded = [vm((rows, n_loc), BF16), DMA, vm(scales.shape, F32), DMA]
    work = 2 * rows * per_row * n_loc * width

    depth = time * t_loc // width
    (mix,) = call(
        spread,
        [(array(owners, depth, width), HBM)],
        [(kernel, HBM)],
        [vm(kernel.shape, BF16), vm((depth, width), BF16), DMA((owners,)), DMA],
    )
    mix = exchange(mix)
    inv, *packs = call(
        first_scale,
        [(scales, HBM), *packed],
        [(xs, HBM), (weights, HBM), (send_list, SMEM), (cheb_coef, SMEM)],
        [loaded[0], vm(weights.shape, BF16), loaded[2], held, DMA((ways,)), DMA((blocks,)), DMA],
        flops=work // 8,
    )
    received = swap(packs)
    term, *packs = call(
        first_product,
        [(field, HBM), *packed],
        [
            (xs, HBM),
            *((r, VMEM) for r in received),
            (weights, VMEM),
            (inv, HBM),
            (col_ref, SMEM),
            (send_list, SMEM),
        ],
        [source, whole, held, DMA((blocks,)), DMA((ways,)), *loaded],
        flops=work,
    )
    (mixed,) = call(
        second_product,
        [(field, HBM)],
        [
            (xs, HBM),
            *((r, VMEM) for r in swap(packs)),
            (weights, VMEM),
            (inv, HBM),
            (col_ref, SMEM),
            (term, HBM),
        ],
        [source, whole, whole, DMA((blocks,)), DMA, *loaded],
        flops=work,
    )
    (filtered,) = call(
        functools.partial(temporal, t_loc),
        [(array(owners, rows, width), HBM)],
        [(exchange(mixed), VMEM), (mix, VMEM)],
        [vm((time, probes * width), BF16), whole, vm((time, time), BF16), DMA((pieces,))],
        flops=2 * time * time * probes * width,
    )
    (out,) = call(unblock, [(array(rows, n_loc), HBM)], [(exchange(filtered), VMEM)], [DMA((blocks,))])
    return out.reshape(probes, t_loc, n_loc)


def solution(mesh):
    in_specs = (
        P(None, "tm", "dom"),
        P("dom", None, None, None),
        P("dom", None, None),
        P("dom", None),
        P("tm", None),
        P(),
    )
    out_specs = P(None, "tm", "dom")
    return jax.shard_map(body, mesh=mesh, in_specs=in_specs, out_specs=out_specs, check_vma=False)
```

```python
import functools

import jax
import jax.numpy as jnp
from jax import lax
from jax.experimental import pallas as pl
from jax.experimental.pallas import tpu as pltpu
from jax.sharding import PartitionSpec as P

REACH = 2
OFFSETS = tuple(range(-REACH, 0)) + tuple(range(1, REACH + 1))
F32, BF16 = jnp.float32, jnp.bfloat16
LIMIT = 24 * 2**20
SMEM = pl.BlockSpec(memory_space=pltpu.SMEM)
VMEM = pl.BlockSpec(memory_space=pltpu.VMEM)
HBM = pl.BlockSpec(memory_space=pltpu.HBM)
DMA = pltpu.SemaphoreType.DMA


def call(kernel, outs, ins, scratch, flops=0, aliases=None):
    arrays, specs = zip(*ins)
    shapes, results = zip(*outs)
    size = sum(a.size * a.dtype.itemsize for a in (*arrays, *shapes))
    arrays = [pltpu.with_memory_space_constraint(a, pltpu.HBM) if spec is HBM else a for a, spec in ins]
    shapes = [pltpu.HBM(a.shape, a.dtype) if spec is HBM else a for a, spec in outs]
    return pl.pallas_call(
        kernel,
        out_shape=shapes,
        in_specs=specs,
        out_specs=results,
        scratch_shapes=scratch,
        compiler_params=pltpu.CompilerParams(vmem_limit_bytes=LIMIT),
        cost_estimate=pl.CostEstimate(flops=flops, bytes_accessed=size, transcendentals=0),
        input_output_aliases=aliases or {},
    )(*arrays)


def array(*shape, dtype=BF16):
    return jax.ShapeDtypeStruct(shape, dtype)


def start(source, target, sem):
    copy = pltpu.make_async_copy(source, target, sem)
    copy.start()
    return copy


def wait(copies):
    for copy in copies:
        copy.wait()


def times_transposed(a, b):
    return lax.dot_general(a, b, (((1,), (1,)), ((), ())), preferred_element_type=F32)


def block_of(ref, g, width):
    if len(ref.shape) == 3:
        return ref[g]
    at = g * width
    return ref[:, pl.ds(at if isinstance(g, int) else pl.multiple_of(at, width), width)]


def scaled_block(ref, inv_ref, g, width):
    return (block_of(ref, g, width).astype(F32) * inv_ref[pl.ds(g, 1), :]).astype(BF16)


def partner_ways():
    place = lax.axis_index("dom")
    odd = lax.rem(place, 2)
    upper = lax.div(lax.rem(place, 4), 2)
    return [2 - odd, 1 + odd, 3 * (1 - upper), 3 * upper]


def partners(index, count):
    reach = 1 + index // 2
    down = [(p // reach) % 2 != index % 2 for p in range(count)]
    return [(p, (p - reach if down[p] else p + reach) % count) for p in range(count)]


def pack(send_ref, field_ref, inv_ref, packs, held, sems):
    width = inv_ref.shape[1]
    copies = []
    ways = partner_ways()
    for i, out in enumerate(packs):
        way = len(OFFSETS) - 1 - ways[i]
        for slot in range(out.shape[0]):
            held[i, slot] = scaled_block(field_ref, inv_ref, send_ref[0, way, slot], width)
        copies.append(start(held.at[i], out, sems.at[i]))
    return copies


def lay_out(signal_ref, kernel_ref, out_ref, held, mix, in_sems, out_sems, mix_sem):
    owners, chunk, width = out_ref.shape
    t_loc, time = kernel_ref.shape
    rows = chunk - time * t_loc // width
    mixing = start(kernel_ref, mix, mix_sem)
    loads = [
        start(signal_ref.at[:rows, i * width : (i + 1) * width], held.at[i, :rows], in_sems.at[i])
        for i in range(owners)
    ]
    mixing.wait()
    copies = []
    for i in range(owners):
        for q in range(time // width):
            held[i, rows + q * t_loc : rows + (q + 1) * t_loc] = mix[:, q * width : (q + 1) * width]
        loads[i].wait()
        copies.append(start(held.at[i], out_ref.at[i], out_sems.at[i]))
    wait(copies)


def first_scale(signal_ref, weights_ref, send_ref, coef_ref, inv_ref, *rest):
    *packs, field, held, sems, load_sem = rest
    blocks, per_row, width, _ = weights_ref.shape
    rows = field.shape[0]
    load = start(signal_ref.at[rows:], field, load_sem)
    ones = jnp.ones((16, width), BF16)
    for g in range(blocks):
        degree = times_transposed(ones, weights_ref[g, 0])
        for j in range(1, per_row):
            degree += times_transposed(ones, weights_ref[g, j])
        inv_ref[g : g + 1, :] = lax.rsqrt(degree[:1])
    for term in range(coef_ref.shape[0]):
        inv_ref[blocks + term : blocks + term + 1, :] = jnp.full((1, width), coef_ref[term], F32)
    load.wait()
    wait(pack(send_ref, field, inv_ref, packs, held, sems))


def scale(field_ref, inv_ref, send_ref, *rest):
    *packs, held, sems = rest
    wait(pack(send_ref, field_ref, inv_ref, packs, held, sems))


def place_received(blocks, received, source):
    for way, ref in zip(partner_ways(), received):
        slots = ref.shape[0]
        for slot in range(slots):
            source[blocks + way * slots + slot] = ref[slot]


def place_own(blocks, field_ref, inv_ref, source):
    for g in range(blocks):
        source[g] = scaled_block(field_ref, inv_ref, g, inv_ref.shape[1])


def block_product(g, col_ref, weights_ref, source):
    per_row = weights_ref.shape[1]
    picked = jnp.concatenate([source[col_ref[g, j]] for j in range(per_row)], axis=1)
    edges = jnp.concatenate([weights_ref[g, j] for j in range(per_row)], axis=1)
    return times_transposed(picked, edges)


def load_half(field_ref, field, sem):
    return [start(field_ref.at[field.shape[0] :], field, sem)]


def first_product(in_hbm, field_ref, r0, r1, r2, r3, weights_ref, inv_ref, col_ref, send_ref, term_ref, *rest):
    *packs, source, term, held, sems, pack_sems = rest[: len(OFFSETS) + 5]
    loads = []
    if in_hbm:
        field, load_sem = rest[len(OFFSETS) + 5 :]
        loads = load_half(field_ref, field, load_sem)
        field_ref = field
    blocks = weights_ref.shape[0]
    place_received(blocks, (r0, r1, r2, r3), source)
    wait(loads)
    place_own(blocks, field_ref, inv_ref, source)
    copies = []
    for g in range(blocks):
        total = block_product(g, col_ref, weights_ref, source)
        term[g] = (-inv_ref[g : g + 1, :] * total).astype(BF16)
        copies.append(start(term.at[g], term_ref.at[g], sems.at[g]))
    wait(copies + pack(send_ref, term, inv_ref, packs, held, pack_sems))


def second_product(in_hbm, field_ref, r0, r1, r2, r3, weights_ref, inv_ref, col_ref, term_ref, out_ref, *rest):
    source, term, held, sems, term_sem = rest[:5]
    loads = [start(term_ref, term, term_sem)]
    if in_hbm:
        field, load_sem = rest[5:]
        loads += load_half(field_ref, field, load_sem)
        field_ref = field
    blocks, _, width, _ = weights_ref.shape
    rows = term.shape[1]
    place_received(blocks, (r0, r1, r2, r3), source)
    wait(loads)
    place_own(blocks, term, inv_ref, source)
    coef = [inv_ref[blocks + i : blocks + i + 1, :] for i in range(3)]
    copies = []
    for g in range(blocks):
        total = block_product(g, col_ref, weights_ref, source)
        x = block_of(field_ref, g, width).astype(F32)
        two = (-2.0 * inv_ref[g : g + 1, :] * total - x).astype(BF16).astype(F32)
        one = term[g].astype(F32)
        held[g] = (coef[0] * x + coef[1] * one + coef[2] * two).astype(BF16)
        if len(out_ref.shape) == 3:
            target = out_ref.at[g]
        else:
            target = out_ref.at[:rows, g * width : (g + 1) * width]
        copies.append(start(held.at[g], target, sems.at[g]))
    wait(copies)


def mix_times(t_loc, mix, field_ref, out_ref, columns, held, sems):
    owners, rows, width = out_ref.shape
    for p in range(rows // t_loc):
        part = slice(p * t_loc, (p + 1) * t_loc)
        for i in range(owners):
            columns[i * t_loc : (i + 1) * t_loc, p * width : (p + 1) * width] = field_ref[i, part]
    step = 2 * width
    pieces = columns.shape[1] // step
    depth = rows // pieces
    copies = []
    for c in range(pieces):
        out = jnp.dot(mix, columns[:, c * step : (c + 1) * step], preferred_element_type=F32).astype(BF16)
        for q in range(step // width):
            at = c * depth + q * t_loc
            for i in range(owners):
                held[i, at : at + t_loc] = out[i * t_loc : (i + 1) * t_loc, q * width : (q + 1) * width]
        part = slice(c * depth, (c + 1) * depth)
        copies.append(start(held.at[:, part], out_ref.at[:, part], sems.at[c]))
    return copies


def first_temporal(t_loc, field_ref, out_ref, mix_ref, columns, held, mix, sems, mix_sem):
    owners, rows, width = out_ref.shape
    for i in range(owners):
        for q in range(mix.shape[1] // width):
            mix[i * t_loc : (i + 1) * t_loc, q * width : (q + 1) * width] = field_ref[
                i, rows + q * t_loc : rows + (q + 1) * t_loc
            ]
    keep = start(mix, mix_ref, mix_sem)
    wait(mix_times(t_loc, mix[...], field_ref, out_ref, columns, held, sems) + [keep])


def second_temporal(t_loc, field_ref, mix_ref, out_ref, columns, held, mix, sems, mix_sem):
    start(mix_ref, mix, mix_sem).wait()
    wait(mix_times(t_loc, mix[...], field_ref, out_ref, columns, held, sems))


def unblock(_, field_ref, out_ref, sems):
    blocks, rows, width = field_ref.shape
    wait(
        [
            start(field_ref.at[g], out_ref.at[rows:, g * width : (g + 1) * width], sems.at[g])
            for g in range(blocks)
        ]
    )


def swap(block, index):
    return lax.ppermute(block, "dom", partners(index, lax.axis_size("dom")))


def exchange(field):
    return lax.all_to_all(field, "tm", split_axis=0, concat_axis=0, tiled=True)


def begin(packs):
    near = [swap(packs[i], i) for i in range(2)]

    def finish(field):
        field, *rest = lax.optimization_barrier((field, *near, *packs[2:]))
        field = exchange(field)
        return field, rest[:2] + [swap(block, 2 + i) for i, block in enumerate(rest[2:])]

    return finish


def body(signal, weights, send_list, col_ref, kernel, cheb_coef):
    probes, t_loc, n_loc = signal.shape
    blocks, per_row, width, _ = weights.shape
    rows = probes * t_loc // 2
    slots = send_list.shape[2]
    owners = lax.axis_size("tm")
    time = kernel.shape[1]
    ways = len(OFFSETS)
    pieces = rows // t_loc // 2
    xs = signal.reshape(2 * rows, n_loc)
    field = array(blocks, rows, width)
    packed = [(array(slots, rows, width), HBM)] * ways
    vm = pltpu.VMEM
    source = vm((blocks + ways * slots, rows, width), BF16)
    whole = vm((blocks, rows, width), BF16)
    held = vm((ways, slots, rows, width), BF16)
    second_half = [vm((rows, n_loc), BF16), DMA]
    mixer = [vm((time, rows // t_loc * width), BF16), whole, vm((time, time), BF16), DMA((pieces,)), DMA]
    work = 2 * rows * per_row * n_loc * width
    mixing = 2 * time * time * rows // t_loc * width

    def one(x, received, inv, in_hbm):
        term, *packs = call(
            functools.partial(first_product, in_hbm),
            [(field, HBM), *packed],
            [
                (x, HBM if in_hbm else VMEM),
                *((r, VMEM) for r in received),
                (weights, VMEM),
                (inv, VMEM),
                (col_ref, SMEM),
                (send_list, SMEM),
            ],
            [source, whole, held, DMA((blocks,)), DMA((ways,))] + (second_half if in_hbm else []),
            flops=work,
        )
        return term, packs

    def two(x, received, inv, term, out, in_hbm):
        return call(
            functools.partial(second_product, in_hbm),
            [(out, HBM)],
            [
                (x, HBM if in_hbm else VMEM),
                *((r, VMEM) for r in received),
                (weights, VMEM),
                (inv, VMEM),
                (col_ref, SMEM),
                (term, HBM),
            ],
            [source, whole, whole, DMA((blocks,)), DMA] + (second_half if in_hbm else []),
            flops=work,
        )[0]

    chunk = rows + time * t_loc // width
    (laid,) = call(
        lay_out,
        [(array(owners, chunk, width), HBM)],
        [(xs, HBM), (kernel, HBM)],
        [vm((owners, chunk, width), BF16), vm(kernel.shape, BF16), DMA((owners,)), DMA((owners,)), DMA],
    )
    arrived = exchange(laid)
    inv, *packs = call(
        first_scale,
        [(array(blocks + 8, width, dtype=F32), VMEM), *packed],
        [(xs, HBM), (weights, VMEM), (send_list, SMEM), (cheb_coef, SMEM)],
        [vm((rows, n_loc), BF16), held, DMA((ways,)), DMA],
        flops=work // 8,
    )
    received = [swap(block, i) for i, block in enumerate(packs)]
    term, packs = one(xs, received, inv, True)

    finish = begin(packs)
    early, mix = call(
        functools.partial(first_temporal, t_loc),
        [(field, HBM), (array(time, time), HBM)],
        [(arrived, VMEM)],
        mixer,
        flops=mixing,
    )
    early, received = finish(early)

    packs = call(scale, packed, [(early, VMEM), (inv, VMEM), (send_list, SMEM)], [held, DMA((ways,))])
    finish = begin(packs)
    late = two(xs, received, inv, term, field, True)
    late, received = finish(late)
    term, packs = one(early, received, inv, False)

    finish = begin(packs)
    (late,) = call(
        functools.partial(second_temporal, t_loc), [(field, HBM)], [(late, VMEM), (mix, HBM)], mixer, flops=mixing
    )
    late, received = finish(late)
    out = array(2 * rows, n_loc)
    done = two(early, received, inv, term, out, False)
    (done,) = call(unblock, [(out, HBM)], [(done, HBM), (late, VMEM)], [DMA((blocks,))], aliases={0: 0})
    return done.reshape(probes, t_loc, n_loc)


def solution(mesh):
    in_specs = (
        P(None, "tm", "dom"),
        P("dom", None, None, None),
        P("dom", None, None),
        P("dom", None),
        P("tm", None),
        P(),
    )
    out_specs = P(None, "tm", "dom")
    return jax.shard_map(body, mesh=mesh, in_specs=in_specs, out_specs=out_specs, check_vma=False)
```

```python
import functools

import jax
import jax.numpy as jnp
from jax import lax
from jax.experimental import pallas as pl
from jax.experimental.pallas import tpu as pltpu
from jax.sharding import PartitionSpec as P

REACH = 2
OFFSETS = tuple(range(-REACH, 0)) + tuple(range(1, REACH + 1))
F32, BF16 = jnp.float32, jnp.bfloat16
LIMIT = 24 * 2**20
SMEM = pl.BlockSpec(memory_space=pltpu.SMEM)
VMEM = pl.BlockSpec(memory_space=pltpu.VMEM)
HBM = pl.BlockSpec(memory_space=pltpu.HBM)
DMA = pltpu.SemaphoreType.DMA


def call(kernel, outs, ins, scratch, flops=0, aliases=None):
    arrays, specs = zip(*ins)
    shapes, results = zip(*outs)
    size = sum(a.size * a.dtype.itemsize for a in (*arrays, *shapes))
    arrays = [pltpu.with_memory_space_constraint(a, pltpu.HBM) if spec is HBM else a for a, spec in ins]
    shapes = [pltpu.HBM(a.shape, a.dtype) if spec is HBM else a for a, spec in outs]
    return pl.pallas_call(
        kernel,
        out_shape=shapes,
        in_specs=specs,
        out_specs=results,
        scratch_shapes=scratch,
        compiler_params=pltpu.CompilerParams(vmem_limit_bytes=LIMIT),
        cost_estimate=pl.CostEstimate(flops=flops, bytes_accessed=size, transcendentals=0),
        input_output_aliases=aliases or {},
    )(*arrays)


def array(*shape, dtype=BF16):
    return jax.ShapeDtypeStruct(shape, dtype)


def start(source, target, sem):
    copy = pltpu.make_async_copy(source, target, sem)
    copy.start()
    return copy


def wait(copies):
    for copy in copies:
        copy.wait()


def times_transposed(a, b):
    return lax.dot_general(a, b, (((1,), (1,)), ((), ())), preferred_element_type=F32)


def block_of(ref, g, width):
    if len(ref.shape) == 3:
        return ref[g]
    at = g * width
    return ref[:, pl.ds(at if isinstance(g, int) else pl.multiple_of(at, width), width)]


def scaled_block(ref, inv_ref, g, width):
    return (block_of(ref, g, width).astype(F32) * inv_ref[pl.ds(g, 1), :]).astype(BF16)


def partner_ways():
    place = lax.axis_index("dom")
    return [0, 1, 2, 3]


def partners(index, count):
    return [(i, (i - OFFSETS[index]) % count) for i in range(count)]


def pack(send_ref, field_ref, inv_ref, packs, held, sems):
    width = inv_ref.shape[1]
    copies = []
    ways = partner_ways()
    for i, out in enumerate(packs):
        way = ways[i]
        for slot in range(out.shape[0]):
            held[i, slot] = scaled_block(field_ref, inv_ref, send_ref[0, way, slot], width)
        copies.append(start(held.at[i], out, sems.at[i]))
    return copies


def lay_out(signal_ref, kernel_ref, out_ref, held, mix, in_sems, out_sems, mix_sem):
    owners, chunk, width = out_ref.shape
    t_loc, time = kernel_ref.shape
    rows = chunk - time * t_loc // width
    mixing = start(kernel_ref, mix, mix_sem)
    loads = [
        start(signal_ref.at[:rows, i * width : (i + 1) * width], held.at[i, :rows], in_sems.at[i])
        for i in range(owners)
    ]
    mixing.wait()
    copies = []
    for i in range(owners):
        for q in range(time // width):
            held[i, rows + q * t_loc : rows + (q + 1) * t_loc] = mix[:, q * width : (q + 1) * width]
        loads[i].wait()
        copies.append(start(held.at[i], out_ref.at[i], out_sems.at[i]))
    wait(copies)


def first_scale(signal_ref, weights_ref, send_ref, coef_ref, inv_ref, *rest):
    *packs, field, held, sems, load_sem = rest
    blocks, per_row, width, _ = weights_ref.shape
    rows = field.shape[0]
    load = start(signal_ref.at[rows:], field, load_sem)
    ones = jnp.ones((16, width), BF16)
    for g in range(blocks):
        degree = times_transposed(ones, weights_ref[g, 0])
        for j in range(1, per_row):
            degree += times_transposed(ones, weights_ref[g, j])
        inv_ref[g : g + 1, :] = lax.rsqrt(degree[:1])
    for term in range(coef_ref.shape[0]):
        inv_ref[blocks + term : blocks + term + 1, :] = jnp.full((1, width), coef_ref[term], F32)
    load.wait()
    wait(pack(send_ref, field, inv_ref, packs, held, sems))


def place_received(blocks, received, source):
    for way, ref in zip(partner_ways(), received):
        slots = ref.shape[0]
        for slot in range(slots):
            source[blocks + way * slots + slot] = ref[slot]


def place_own(blocks, field_ref, inv_ref, source):
    for g in range(blocks):
        source[g] = scaled_block(field_ref, inv_ref, g, inv_ref.shape[1])


def block_product(g, col_ref, weights_ref, source):
    per_row = weights_ref.shape[1]
    picked = jnp.concatenate([source[col_ref[g, j]] for j in range(per_row)], axis=1)
    edges = jnp.concatenate([weights_ref[g, j] for j in range(per_row)], axis=1)
    return times_transposed(picked, edges)


def product_one(field, received, weights_ref, inv_ref, col_ref, send_ref, term_ref, packs, scratch, loads):
    source, term, held, sems, pack_sems = scratch
    blocks = weights_ref.shape[0]
    place_received(blocks, received, source)
    wait(loads)
    place_own(blocks, field, inv_ref, source)
    copies = []
    for g in range(blocks):
        total = block_product(g, col_ref, weights_ref, source)
        term[g] = (-inv_ref[g : g + 1, :] * total).astype(BF16)
        copies.append(start(term.at[g], term_ref.at[g], sems.at[g]))
    return copies + pack(send_ref, term, inv_ref, packs, held, pack_sems)


def product_two(field, received, weights_ref, inv_ref, col_ref, term_ref, target, scratch, loads):
    source, term, mixed, sems, term_sem = scratch
    start_term = start(term_ref, term, term_sem)
    blocks, _, width, _ = weights_ref.shape
    place_received(blocks, received, source)
    start_term.wait()
    place_own(blocks, term, inv_ref, source)
    coef = [inv_ref[blocks + i : blocks + i + 1, :] for i in range(3)]
    wait(loads)
    copies = []
    for g in range(blocks):
        total = block_product(g, col_ref, weights_ref, source)
        x = block_of(field, g, width).astype(F32)
        two = (-2.0 * inv_ref[g : g + 1, :] * total - x).astype(BF16).astype(F32)
        one = term[g].astype(F32)
        mixed[g] = (coef[0] * x + coef[1] * one + coef[2] * two).astype(BF16)
        copies.append(start(mixed.at[g], target(g), sems.at[g]))
    return copies


def mix_times(t_loc, mix, field_ref, out_ref, columns, held, sems):
    owners, rows, width = out_ref.shape
    for p in range(rows // t_loc):
        part = slice(p * t_loc, (p + 1) * t_loc)
        for i in range(owners):
            columns[i * t_loc : (i + 1) * t_loc, p * width : (p + 1) * width] = field_ref[i, part]
    step = 2 * width
    pieces = columns.shape[1] // step
    depth = rows // pieces
    copies = []
    for c in range(pieces):
        out = jnp.dot(mix, columns[:, c * step : (c + 1) * step], preferred_element_type=F32).astype(BF16)
        for q in range(step // width):
            at = c * depth + q * t_loc
            for i in range(owners):
                held[i, at : at + t_loc] = out[i * t_loc : (i + 1) * t_loc, q * width : (q + 1) * width]
        part = slice(c * depth, (c + 1) * depth)
        copies.append(start(held.at[:, part], out_ref.at[:, part], sems.at[c]))
    return copies


def rear_one(t_loc, signal_ref, r0, r1, r2, r3, weights_ref, inv_ref, col_ref, send_ref, arrived_ref, term_ref, *rest):
    *packs, out_ref, mix_ref = rest[: len(OFFSETS) + 2]
    *scratch, field, columns, mixed, mix, arrived, load_sems, out_sems = rest[len(OFFSETS) + 2 :]
    owners, rows, width = out_ref.shape
    load = start(signal_ref.at[rows:], field, load_sems.at[0])
    loads = [start(arrived_ref.at[i], arrived.at[i], load_sems.at[2 + i]) for i in range(owners)]
    copies = product_one(
        field, (r0, r1, r2, r3), weights_ref, inv_ref, col_ref, send_ref, term_ref, packs, scratch, [load]
    )
    for i in range(owners):
        loads[i].wait()
        for q in range(mix.shape[1] // width):
            mix[i * t_loc : (i + 1) * t_loc, q * width : (q + 1) * width] = arrived[
                i, rows + q * t_loc : rows + (q + 1) * t_loc
            ]
    copies.append(start(mix, mix_ref, load_sems.at[1]))
    wait(copies + mix_times(t_loc, mix[...], arrived, out_ref, columns, mixed, out_sems))


def front_one(t_loc, field_ref, r0, r1, r2, r3, weights_ref, inv_ref, col_ref, send_ref, arrived_ref, mix_ref, term_ref, *rest):
    *packs, out_ref = rest[: len(OFFSETS) + 1]
    *scratch, field, columns, mixed, mix, arrived, load_sems, out_sems = rest[len(OFFSETS) + 1 :]
    load = start(field_ref, field, load_sems.at[0])
    loads = [start(mix_ref, mix, load_sems.at[1]), start(arrived_ref, arrived, load_sems.at[2])]
    copies = product_one(
        field, (r0, r1, r2, r3), weights_ref, inv_ref, col_ref, send_ref, term_ref, packs, scratch, [load]
    )
    wait(loads)
    wait(copies + mix_times(t_loc, mix[...], arrived, out_ref, columns, mixed, out_sems))


def rear_two(signal_ref, r0, r1, r2, r3, weights_ref, inv_ref, col_ref, term_ref, send_ref, early_ref, out_ref, *rest):
    packs = rest[: len(OFFSETS)]
    *scratch, field, early, held, load_sems, pack_sems = rest[len(OFFSETS) :]
    load = start(signal_ref.at[field.shape[0] :], field, load_sems.at[0])
    start(early_ref, early, load_sems.at[1]).wait()
    copies = pack(send_ref, early, inv_ref, packs, held, pack_sems)
    wait(
        copies
        + product_two(
            field, (r0, r1, r2, r3), weights_ref, inv_ref, col_ref, term_ref, lambda g: out_ref.at[g], scratch, [load]
        )
    )


def front_two(field_ref, r0, r1, r2, r3, weights_ref, inv_ref, col_ref, term_ref, late_ref, out_ref, *rest):
    *scratch, field, late, load_sems, late_sems = rest
    blocks, rows, width = late.shape
    load = start(field_ref, field, load_sems.at[0])
    loads = [start(late_ref, late, load_sems.at[1])]

    def target(g):
        return out_ref.at[:rows, g * width : (g + 1) * width]

    copies = product_two(
        field, (r0, r1, r2, r3), weights_ref, inv_ref, col_ref, term_ref, target, scratch, [load]
    )
    wait(loads)
    copies += [
        start(late.at[g], out_ref.at[rows:, g * width : (g + 1) * width], late_sems.at[g]) for g in range(blocks)
    ]
    wait(copies)


def swap(packs):
    count = lax.axis_size("dom")
    return [lax.ppermute(block, "dom", partners(i, count)) for i, block in enumerate(packs)]


def exchange(field):
    return lax.all_to_all(field, "tm", split_axis=0, concat_axis=0, tiled=True)


def body(signal, weights, send_list, col_ref, kernel, cheb_coef):
    probes, t_loc, n_loc = signal.shape
    blocks, per_row, width, _ = weights.shape
    rows = probes * t_loc // 2
    slots = send_list.shape[2]
    owners = lax.axis_size("tm")
    time = kernel.shape[1]
    ways = len(OFFSETS)
    pieces = rows // t_loc // 2
    xs = signal.reshape(2 * rows, n_loc)
    field = array(blocks, rows, width)
    packed = [(array(slots, rows, width), HBM)] * ways
    vm = pltpu.VMEM
    source = vm((blocks + ways * slots, rows, width), BF16)
    whole = vm((blocks, rows, width), BF16)
    held = vm((ways, slots, rows, width), BF16)
    columns = vm((time, rows // t_loc * width), BF16)
    square = vm((time, time), BF16)
    scratch_one = [source, whole, held, DMA((blocks,)), DMA((ways,))]
    scratch_two = [source, whole, whole, DMA((blocks,)), DMA]
    side_by_side = vm((rows, n_loc), BF16)
    work = 2 * rows * per_row * n_loc * width
    mixing = 2 * time * time * rows // t_loc * width

    def operands(x, packs, inv):
        received = [(r, VMEM) for r in swap(packs)]
        return [(x, HBM), *received, (weights, VMEM), (inv, VMEM), (col_ref, SMEM)]

    chunk = rows + time * t_loc // width
    (laid,) = call(
        lay_out,
        [(array(owners, chunk, width), HBM)],
        [(xs, HBM), (kernel, HBM)],
        [vm((owners, chunk, width), BF16), vm(kernel.shape, BF16), DMA((owners,)), DMA((owners,)), DMA],
    )
    arrived = exchange(laid)
    inv, *packs = call(
        first_scale,
        [(array(blocks + 8, width, dtype=F32), VMEM), *packed],
        [(xs, HBM), (weights, VMEM), (send_list, SMEM), (cheb_coef, SMEM)],
        [side_by_side, held, DMA((ways,)), DMA],
        flops=work // 8,
    )
    term, *packs, early, mix = call(
        functools.partial(rear_one, t_loc),
        [(field, HBM), *packed, (field, HBM), (array(time, time), HBM)],
        [*operands(xs, packs, inv), (send_list, SMEM), (arrived, HBM)],
        [*scratch_one, side_by_side, columns, whole, square, vm(laid.shape, BF16), DMA((2 + owners,)), DMA((pieces,))],
        flops=work + mixing,
    )
    early = exchange(early)
    late, *front = call(
        rear_two,
        [(field, HBM), *packed],
        [*operands(xs, packs, inv), (term, HBM), (send_list, SMEM), (early, HBM)],
        [*scratch_two, side_by_side, whole, held, DMA((2,)), DMA((ways,))],
        flops=work,
    )
    late = exchange(late)
    term, *packs, late = call(
        functools.partial(front_one, t_loc),
        [(field, HBM), *packed, (field, HBM)],
        [*operands(early, front, inv), (send_list, SMEM), (late, HBM), (mix, HBM)],
        [*scratch_one, whole, columns, whole, square, whole, DMA((3,)), DMA((pieces,))],
        flops=work + mixing,
    )
    late = exchange(late)
    (out,) = call(
        front_two,
        [(array(2 * rows, n_loc), HBM)],
        [*operands(early, packs, inv), (term, HBM), (late, HBM)],
        [*scratch_two, whole, whole, DMA((2,)), DMA((blocks,))],
        flops=work,
    )
    return out.reshape(probes, t_loc, n_loc)


def solution(mesh):
    in_specs = (
        P(None, "tm", "dom"),
        P("dom", None, None, None),
        P("dom", None, None),
        P("dom", None),
        P("tm", None),
        P(),
    )
    out_specs = P(None, "tm", "dom")
    return jax.shard_map(body, mesh=mesh, in_specs=in_specs, out_specs=out_specs, check_vma=False)
```

```python
import functools

import jax
import jax.numpy as jnp
from jax import lax
from jax.experimental import pallas as pl
from jax.experimental.pallas import tpu as pltpu
from jax.sharding import PartitionSpec as P

REACH = 2
OFFSETS = tuple(range(-REACH, 0)) + tuple(range(1, REACH + 1))
F32, BF16 = jnp.float32, jnp.bfloat16
LIMIT = 24 * 2**20
SMEM = pl.BlockSpec(memory_space=pltpu.SMEM)
VMEM = pl.BlockSpec(memory_space=pltpu.VMEM)
HBM = pl.BlockSpec(memory_space=pltpu.HBM)
DMA = pltpu.SemaphoreType.DMA


def call(kernel, outs, ins, scratch, flops=0, aliases=None):
    arrays, specs = zip(*ins)
    shapes, results = zip(*outs)
    size = sum(a.size * a.dtype.itemsize for a in (*arrays, *shapes))
    arrays = [pltpu.with_memory_space_constraint(a, pltpu.HBM) if spec is HBM else a for a, spec in ins]
    shapes = [pltpu.HBM(a.shape, a.dtype) if spec is HBM else a for a, spec in outs]
    return pl.pallas_call(
        kernel,
        out_shape=shapes,
        in_specs=specs,
        out_specs=results,
        scratch_shapes=scratch,
        compiler_params=pltpu.CompilerParams(vmem_limit_bytes=LIMIT),
        cost_estimate=pl.CostEstimate(flops=flops, bytes_accessed=size, transcendentals=0),
        input_output_aliases=aliases or {},
    )(*arrays)


def array(*shape, dtype=BF16):
    return jax.ShapeDtypeStruct(shape, dtype)


def start(source, target, sem):
    copy = pltpu.make_async_copy(source, target, sem)
    copy.start()
    return copy


def wait(copies):
    for copy in copies:
        copy.wait()


def times_transposed(a, b):
    return lax.dot_general(a, b, (((1,), (1,)), ((), ())), preferred_element_type=F32)


def block_of(ref, g, width):
    if len(ref.shape) == 3:
        return ref[g]
    at = g * width
    return ref[:, pl.ds(at if isinstance(g, int) else pl.multiple_of(at, width), width)]


def scaled_block(ref, inv_ref, g, width):
    return (block_of(ref, g, width).astype(F32) * inv_ref[pl.ds(g, 1), :]).astype(BF16)


def partner_ways():
    place = lax.axis_index("dom")
    return [0, 1, 2, 3]


def partners(index, count):
    return [(i, (i - OFFSETS[index]) % count) for i in range(count)]


def pack(send_ref, field_ref, inv_ref, packs, held, sems):
    width = inv_ref.shape[1]
    copies = []
    ways = partner_ways()
    for i, out in enumerate(packs):
        way = ways[i]
        for slot in range(out.shape[0]):
            held[i, slot] = scaled_block(field_ref, inv_ref, send_ref[0, way, slot], width)
        copies.append(start(held.at[i], out, sems.at[i]))
    return copies


def lay_out(signal_ref, kernel_ref, out_ref, held, mix, in_sems, out_sems, mix_sem):
    owners, chunk, width = out_ref.shape
    t_loc, time = kernel_ref.shape
    rows = chunk - time * t_loc // width
    mixing = start(kernel_ref, mix, mix_sem)
    loads = [
        start(signal_ref.at[:rows, i * width : (i + 1) * width], held.at[i, :rows], in_sems.at[i])
        for i in range(owners)
    ]
    mixing.wait()
    copies = []
    for i in range(owners):
        for q in range(time // width):
            held[i, rows + q * t_loc : rows + (q + 1) * t_loc] = mix[:, q * width : (q + 1) * width]
        loads[i].wait()
        copies.append(start(held.at[i], out_ref.at[i], out_sems.at[i]))
    wait(copies)


def first_scale(signal_ref, weights_ref, send_ref, coef_ref, inv_ref, *rest):
    *packs, field, held, sems, load_sem = rest
    blocks, per_row, width, _ = weights_ref.shape
    rows = field.shape[0]
    load = start(signal_ref.at[rows:], field, load_sem)
    ones = jnp.ones((16, width), BF16)
    for g in range(blocks):
        degree = times_transposed(ones, weights_ref[g, 0])
        for j in range(1, per_row):
            degree += times_transposed(ones, weights_ref[g, j])
        inv_ref[g : g + 1, :] = lax.rsqrt(degree[:1])
    for term in range(coef_ref.shape[0]):
        inv_ref[blocks + term : blocks + term + 1, :] = jnp.full((1, width), coef_ref[term], F32)
    load.wait()
    wait(pack(send_ref, field, inv_ref, packs, held, sems))


def place_received(blocks, received, source):
    for way, ref in zip(partner_ways(), received):
        slots = ref.shape[0]
        for slot in range(slots):
            source[blocks + way * slots + slot] = ref[slot]


def place_own(blocks, field_ref, inv_ref, source):
    for g in range(blocks):
        source[g] = scaled_block(field_ref, inv_ref, g, inv_ref.shape[1])


def block_product(g, col_ref, weights_ref, source):
    per_row = weights_ref.shape[1]
    picked = jnp.concatenate([source[col_ref[g, j]] for j in range(per_row)], axis=1)
    edges = jnp.concatenate([weights_ref[g, j] for j in range(per_row)], axis=1)
    return times_transposed(picked, edges)


def product_one(field, received, weights_ref, inv_ref, col_ref, send_ref, term_ref, packs, scratch, loads):
    source, term, held, sems, pack_sems = scratch
    blocks = weights_ref.shape[0]
    place_received(blocks, received, source)
    wait(loads)
    place_own(blocks, field, inv_ref, source)
    copies = []
    for g in range(blocks):
        total = block_product(g, col_ref, weights_ref, source)
        term[g] = (-inv_ref[g : g + 1, :] * total).astype(BF16)
        copies.append(start(term.at[g], term_ref.at[g], sems.at[g]))
    return copies + pack(send_ref, term, inv_ref, packs, held, pack_sems)


def product_two(field, received, weights_ref, inv_ref, col_ref, term_ref, target, scratch, loads):
    source, term, mixed, sems, term_sem = scratch
    start_term = start(term_ref, term, term_sem)
    blocks, _, width, _ = weights_ref.shape
    place_received(blocks, received, source)
    start_term.wait()
    place_own(blocks, term, inv_ref, source)
    coef = [inv_ref[blocks + i : blocks + i + 1, :] for i in range(3)]
    wait(loads)
    copies = []
    for g in range(blocks):
        total = block_product(g, col_ref, weights_ref, source)
        x = block_of(field, g, width).astype(F32)
        two = (-2.0 * inv_ref[g : g + 1, :] * total - x).astype(BF16).astype(F32)
        one = term[g].astype(F32)
        mixed[g] = (coef[0] * x + coef[1] * one + coef[2] * two).astype(BF16)
        copies.append(start(mixed.at[g], target(g), sems.at[g]))
    return copies


def mix_times(t_loc, mix, field_ref, out_ref, columns, held, sems):
    owners, rows, width = out_ref.shape
    for p in range(rows // t_loc):
        part = slice(p * t_loc, (p + 1) * t_loc)
        for i in range(owners):
            columns[i * t_loc : (i + 1) * t_loc, p * width : (p + 1) * width] = field_ref[i, part]
    step = 2 * width
    pieces = columns.shape[1] // step
    depth = rows // pieces
    copies = []
    for c in range(pieces):
        out = jnp.dot(mix, columns[:, c * step : (c + 1) * step], preferred_element_type=F32).astype(BF16)
        for q in range(step // width):
            at = c * depth + q * t_loc
            for i in range(owners):
                held[i, at : at + t_loc] = out[i * t_loc : (i + 1) * t_loc, q * width : (q + 1) * width]
        part = slice(c * depth, (c + 1) * depth)
        copies.append(start(held.at[:, part], out_ref.at[:, part], sems.at[c]))
    return copies


def rear_one(t_loc, signal_ref, r0, r1, r2, r3, weights_ref, inv_ref, col_ref, send_ref, arrived_ref, term_ref, *rest):
    *packs, out_ref, mix_ref = rest[: len(OFFSETS) + 2]
    *scratch, field, columns, mixed, mix, arrived, load_sems, out_sems = rest[len(OFFSETS) + 2 :]
    owners, rows, width = out_ref.shape
    load = start(signal_ref.at[rows:], field, load_sems.at[0])
    loads = [start(arrived_ref.at[i], arrived.at[i], load_sems.at[2 + i]) for i in range(owners)]
    copies = product_one(
        field, (r0, r1, r2, r3), weights_ref, inv_ref, col_ref, send_ref, term_ref, packs, scratch, [load]
    )
    for i in range(owners):
        loads[i].wait()
        for q in range(mix.shape[1] // width):
            mix[i * t_loc : (i + 1) * t_loc, q * width : (q + 1) * width] = arrived[
                i, rows + q * t_loc : rows + (q + 1) * t_loc
            ]
    copies.append(start(mix, mix_ref, load_sems.at[1]))
    wait(copies + mix_times(t_loc, mix[...], arrived, out_ref, columns, mixed, out_sems))


def front_one(field_ref, r0, r1, r2, r3, weights_ref, inv_ref, col_ref, send_ref, term_ref, *rest):
    packs = rest[: len(OFFSETS)]
    *scratch, field, load_sem = rest[len(OFFSETS) :]
    load = start(field_ref, field, load_sem)
    wait(
        product_one(
            field, (r0, r1, r2, r3), weights_ref, inv_ref, col_ref, send_ref, term_ref, packs, scratch, [load]
        )
    )


def second_temporal(t_loc, arrived_ref, mix_ref, out_ref, columns, mixed, mix, arrived, load_sems, out_sems):
    wait([start(arrived_ref, arrived, load_sems.at[0]), start(mix_ref, mix, load_sems.at[1])])
    wait(mix_times(t_loc, mix[...], arrived, out_ref, columns, mixed, out_sems))


def rear_two(signal_ref, r0, r1, r2, r3, weights_ref, inv_ref, col_ref, term_ref, out_ref, *rest):
    *scratch, field, load_sem = rest
    load = start(signal_ref.at[field.shape[0] :], field, load_sem)
    wait(
        product_two(
            field, (r0, r1, r2, r3), weights_ref, inv_ref, col_ref, term_ref, lambda g: out_ref.at[g], scratch, [load]
        )
    )


def front_packs(early_ref, inv_ref, send_ref, *rest):
    packs = rest[: len(OFFSETS)]
    early, held, load_sem, pack_sems = rest[len(OFFSETS) :]
    start(early_ref, early, load_sem).wait()
    wait(pack(send_ref, early, inv_ref, packs, held, pack_sems))


def front_two(field_ref, r0, r1, r2, r3, weights_ref, inv_ref, col_ref, term_ref, _, out_ref, *rest):
    *scratch, field, load_sem = rest
    rows, width = field.shape[1:]

    def target(g):
        return out_ref.at[:rows, g * width : (g + 1) * width]

    load = start(field_ref, field, load_sem)
    wait(
        product_two(
            field, (r0, r1, r2, r3), weights_ref, inv_ref, col_ref, term_ref, target, scratch, [load]
        )
    )


def unblock(late_ref, out_ref, late, load_sem, sems):
    blocks, rows, width = late.shape
    start(late_ref, late, load_sem).wait()
    wait(
        [start(late.at[g], out_ref.at[rows:, g * width : (g + 1) * width], sems.at[g]) for g in range(blocks)]
    )


def swap(packs):
    count = lax.axis_size("dom")
    return [lax.ppermute(block, "dom", partners(i, count)) for i, block in enumerate(packs)]


def exchange(field):
    return lax.all_to_all(field, "tm", split_axis=0, concat_axis=0, tiled=True)


def body(signal, weights, send_list, col_ref, kernel, cheb_coef):
    probes, t_loc, n_loc = signal.shape
    blocks, per_row, width, _ = weights.shape
    rows = probes * t_loc // 2
    slots = send_list.shape[2]
    owners = lax.axis_size("tm")
    time = kernel.shape[1]
    ways = len(OFFSETS)
    pieces = rows // t_loc // 2
    xs = signal.reshape(2 * rows, n_loc)
    field = array(blocks, rows, width)
    packed = [(array(slots, rows, width), HBM)] * ways
    vm = pltpu.VMEM
    source = vm((blocks + ways * slots, rows, width), BF16)
    whole = vm((blocks, rows, width), BF16)
    held = vm((ways, slots, rows, width), BF16)
    columns = vm((time, rows // t_loc * width), BF16)
    square = vm((time, time), BF16)
    scratch_one = [source, whole, held, DMA((blocks,)), DMA((ways,))]
    scratch_two = [source, whole, whole, DMA((blocks,)), DMA]
    side_by_side = vm((rows, n_loc), BF16)
    work = 2 * rows * per_row * n_loc * width
    mixing = 2 * time * time * rows // t_loc * width

    def operands(x, packs, inv):
        received = [(r, VMEM) for r in swap(packs)]
        return [(x, HBM), *received, (weights, VMEM), (inv, VMEM), (col_ref, SMEM)]

    chunk = rows + time * t_loc // width
    (laid,) = call(
        lay_out,
        [(array(owners, chunk, width), HBM)],
        [(xs, HBM), (kernel, HBM)],
        [vm((owners, chunk, width), BF16), vm(kernel.shape, BF16), DMA((owners,)), DMA((owners,)), DMA],
    )
    arrived = exchange(laid)
    inv, *packs = call(
        first_scale,
        [(array(blocks + 8, width, dtype=F32), VMEM), *packed],
        [(xs, HBM), (weights, VMEM), (send_list, SMEM), (cheb_coef, SMEM)],
        [side_by_side, held, DMA((ways,)), DMA],
        flops=work // 8,
    )
    term, *packs, early, mix = call(
        functools.partial(rear_one, t_loc),
        [(field, HBM), *packed, (field, HBM), (array(time, time), HBM)],
        [*operands(xs, packs, inv), (send_list, SMEM), (arrived, HBM)],
        [*scratch_one, side_by_side, columns, whole, square, vm(laid.shape, BF16), DMA((2 + owners,)), DMA((pieces,))],
        flops=work + mixing,
    )
    early = exchange(early)
    takes = operands(xs, packs, inv)
    front = call(
        front_packs, packed, [(early, HBM), (inv, VMEM), (send_list, SMEM)], [whole, held, DMA, DMA((ways,))]
    )
    term, *front = lax.optimization_barrier((term, *front))
    (late,) = call(
        rear_two, [(field, HBM)], [*takes, (term, HBM)], [*scratch_two, side_by_side, DMA], flops=work
    )
    late, *front = lax.optimization_barrier((late, *front))
    late = exchange(late)
    takes = operands(early, front, inv)
    (late,) = call(
        functools.partial(second_temporal, t_loc),
        [(field, HBM)],
        [(late, HBM), (mix, HBM)],
        [columns, whole, square, whole, DMA((2,)), DMA((pieces,))],
        flops=mixing,
    )
    late, term = lax.optimization_barrier((late, takes[0][0]))
    takes[0] = (term, HBM)
    term, *packs = call(
        front_one, [(field, HBM), *packed], [*takes, (send_list, SMEM)], [*scratch_one, whole, DMA], flops=work
    )
    late, *packs = lax.optimization_barrier((late, *packs))
    late = exchange(late)
    takes = operands(early, packs, inv)
    out = array(2 * rows, n_loc)
    (rear,) = call(unblock, [(out, HBM)], [(late, HBM)], [whole, DMA, DMA((blocks,))])
    (out,) = call(
        front_two,
        [(out, HBM)],
        [*takes, (term, HBM), (rear, HBM)],
        [*scratch_two, whole, DMA],
        flops=work,
        aliases={9: 0},
    )
    return out.reshape(probes, t_loc, n_loc)


def solution(mesh):
    in_specs = (
        P(None, "tm", "dom"),
        P("dom", None, None, None),
        P("dom", None, None),
        P("dom", None),
        P("tm", None),
        P(),
    )
    out_specs = P(None, "tm", "dom")
    return jax.shard_map(body, mesh=mesh, in_specs=in_specs, out_specs=out_specs, check_vma=False)
```

```python
import functools

import jax
import jax.numpy as jnp
from jax import lax
from jax.experimental import pallas as pl
from jax.experimental.pallas import tpu as pltpu
from jax.sharding import PartitionSpec as P

REACH = 2
OFFSETS = tuple(range(-REACH, 0)) + tuple(range(1, REACH + 1))
F32, BF16 = jnp.float32, jnp.bfloat16
LIMIT = 24 * 2**20
SMEM = pl.BlockSpec(memory_space=pltpu.SMEM)
VMEM = pl.BlockSpec(memory_space=pltpu.VMEM)
HBM = pl.BlockSpec(memory_space=pltpu.HBM)
DMA = pltpu.SemaphoreType.DMA


def call(kernel, outs, ins, scratch, flops=0, aliases=None):
    arrays, specs = zip(*ins)
    shapes, results = zip(*outs)
    size = sum(a.size * a.dtype.itemsize for a in (*arrays, *shapes))
    arrays = [pltpu.with_memory_space_constraint(a, pltpu.HBM) if spec is HBM else a for a, spec in ins]
    shapes = [pltpu.HBM(a.shape, a.dtype) if spec is HBM else a for a, spec in outs]
    return pl.pallas_call(
        kernel,
        out_shape=shapes,
        in_specs=specs,
        out_specs=results,
        scratch_shapes=scratch,
        compiler_params=pltpu.CompilerParams(vmem_limit_bytes=LIMIT),
        cost_estimate=pl.CostEstimate(flops=flops, bytes_accessed=size, transcendentals=0),
        input_output_aliases=aliases or {},
    )(*arrays)


def array(*shape, dtype=BF16):
    return jax.ShapeDtypeStruct(shape, dtype)


def start(source, target, sem):
    copy = pltpu.make_async_copy(source, target, sem)
    copy.start()
    return copy


def wait(copies):
    for copy in copies:
        copy.wait()


def ended(g, count):
    size = count // 2
    return slice(g + 1 - size, g + 1) if (g + 1) % size == 0 else None


def times_transposed(a, b):
    return lax.dot_general(a, b, (((1,), (1,)), ((), ())), preferred_element_type=F32)


def block_of(ref, g, width):
    if len(ref.shape) == 3:
        return ref[g]
    at = g * width
    return ref[:, pl.ds(at if isinstance(g, int) else pl.multiple_of(at, width), width)]


def scaled_block(ref, inv_ref, g, width):
    return (block_of(ref, g, width).astype(F32) * inv_ref[pl.ds(g, 1), :]).astype(BF16)


def partner_ways():
    place = lax.axis_index("dom")
    return [0, 1, 2, 3]


def partners(index, count):
    return [(i, (i - OFFSETS[index]) % count) for i in range(count)]


def pack(send_ref, field_ref, inv_ref, packs, held, sems):
    width = inv_ref.shape[1]
    copies = []
    ways = partner_ways()
    for i, out in enumerate(packs):
        way = ways[i]
        for slot in range(out.shape[0]):
            held[i, slot] = scaled_block(field_ref, inv_ref, send_ref[0, way, slot], width)
        copies.append(start(held.at[i], out, sems.at[i]))
    return copies


def lay_out(signal_ref, kernel_ref, out_ref, field, held, mix, sems):
    owners, _, width = out_ref.shape
    t_loc, time = kernel_ref.shape
    rows = field.shape[0]
    mixing = start(kernel_ref, mix, sems.at[0])
    load = start(signal_ref.at[:rows], field, sems.at[1])
    mixing.wait()
    for i in range(owners):
        for q in range(time // width):
            held[i, rows + q * t_loc : rows + (q + 1) * t_loc] = mix[:, q * width : (q + 1) * width]
    load.wait()
    copies = []
    for i in range(owners):
        held[i, :rows] = field[:, i * width : (i + 1) * width]
        if part := ended(i, owners):
            copies.append(start(held.at[part], out_ref.at[part], sems.at[len(copies)]))
    wait(copies)


def first_scale(signal_ref, weights_ref, send_ref, coef_ref, inv_ref, *rest):
    *packs, field, held, sems, load_sem = rest
    blocks, per_row, width, _ = weights_ref.shape
    rows = field.shape[0]
    load = start(signal_ref.at[rows:], field, load_sem)
    ones = jnp.ones((16, width), BF16)
    for g in range(blocks):
        degree = times_transposed(ones, weights_ref[g, 0])
        for j in range(1, per_row):
            degree += times_transposed(ones, weights_ref[g, j])
        inv_ref[g : g + 1, :] = lax.rsqrt(degree[:1])
    for term in range(coef_ref.shape[0]):
        inv_ref[blocks + term : blocks + term + 1, :] = jnp.full((1, width), coef_ref[term], F32)
    load.wait()
    wait(pack(send_ref, field, inv_ref, packs, held, sems))


def place_received(blocks, received, source):
    for way, ref in zip(partner_ways(), received):
        slots = ref.shape[0]
        for slot in range(slots):
            source[blocks + way * slots + slot] = ref[slot]


def place_own(blocks, field_ref, inv_ref, source):
    for g in range(blocks):
        source[g] = scaled_block(field_ref, inv_ref, g, inv_ref.shape[1])


def block_product(g, col_ref, weights_ref, source):
    per_row = weights_ref.shape[1]
    picked = jnp.concatenate([source[col_ref[g, j]] for j in range(per_row)], axis=1)
    edges = jnp.concatenate([weights_ref[g, j] for j in range(per_row)], axis=1)
    return times_transposed(picked, edges)


def product_one(field, received, weights_ref, inv_ref, col_ref, send_ref, term_ref, packs, scratch, loads):
    source, term, held, sems, pack_sems = scratch
    blocks = weights_ref.shape[0]
    place_received(blocks, received, source)
    wait(loads)
    place_own(blocks, field, inv_ref, source)
    copies = []
    for g in range(blocks):
        total = block_product(g, col_ref, weights_ref, source)
        term[g] = (-inv_ref[g : g + 1, :] * total).astype(BF16)
        if part := ended(g, blocks):
            copies.append(start(term.at[part], term_ref.at[part], sems.at[len(copies)]))
    return copies + pack(send_ref, term, inv_ref, packs, held, pack_sems)


def product_two(field, received, weights_ref, inv_ref, col_ref, term_ref, target, scratch, loads):
    source, term, mixed, sems, term_sem = scratch
    start_term = start(term_ref, term, term_sem)
    blocks, _, width, _ = weights_ref.shape
    place_received(blocks, received, source)
    start_term.wait()
    place_own(blocks, term, inv_ref, source)
    coef = [inv_ref[blocks + i : blocks + i + 1, :] for i in range(3)]
    wait(loads)
    copies = []
    for g in range(blocks):
        total = block_product(g, col_ref, weights_ref, source)
        x = block_of(field, g, width).astype(F32)
        two = (-2.0 * inv_ref[g : g + 1, :] * total - x).astype(BF16).astype(F32)
        one = term[g].astype(F32)
        mixed[g] = (coef[0] * x + coef[1] * one + coef[2] * two).astype(BF16)
        copies.append(start(mixed.at[g], target(g), sems.at[g]))
    return copies


def mix_times(t_loc, mix, field_ref, out_ref, columns, held, sems):
    owners, rows, width = out_ref.shape
    for p in range(rows // t_loc):
        part = slice(p * t_loc, (p + 1) * t_loc)
        for i in range(owners):
            columns[i * t_loc : (i + 1) * t_loc, p * width : (p + 1) * width] = field_ref[i, part]
    step = 2 * width
    pieces = columns.shape[1] // step
    depth = rows // pieces
    copies = []
    for c in range(pieces):
        out = jnp.dot(mix, columns[:, c * step : (c + 1) * step], preferred_element_type=F32).astype(BF16)
        for q in range(step // width):
            at = c * depth + q * t_loc
            for i in range(owners):
                held[i, at : at + t_loc] = out[i * t_loc : (i + 1) * t_loc, q * width : (q + 1) * width]
        part = slice(c * depth, (c + 1) * depth)
        copies.append(start(held.at[:, part], out_ref.at[:, part], sems.at[c]))
    return copies


def rear_one(t_loc, signal_ref, r0, r1, r2, r3, weights_ref, inv_ref, col_ref, send_ref, arrived_ref, term_ref, *rest):
    *packs, out_ref, mix_ref = rest[: len(OFFSETS) + 2]
    *scratch, field, columns, mixed, mix, arrived, load_sems, out_sems = rest[len(OFFSETS) + 2 :]
    owners, rows, width = out_ref.shape
    load = start(signal_ref.at[rows:], field, load_sems.at[0])
    load_arrived = start(arrived_ref, arrived, load_sems.at[2])
    copies = product_one(
        field, (r0, r1, r2, r3), weights_ref, inv_ref, col_ref, send_ref, term_ref, packs, scratch, [load]
    )
    load_arrived.wait()
    for i in range(owners):
        for q in range(mix.shape[1] // width):
            mix[i * t_loc : (i + 1) * t_loc, q * width : (q + 1) * width] = arrived[
                i, rows + q * t_loc : rows + (q + 1) * t_loc
            ]
    copies.append(start(mix, mix_ref, load_sems.at[1]))
    wait(copies + mix_times(t_loc, mix[...], arrived, out_ref, columns, mixed, out_sems))


def front_one(field_ref, r0, r1, r2, r3, weights_ref, inv_ref, col_ref, send_ref, term_ref, *rest):
    packs = rest[: len(OFFSETS)]
    *scratch, field, load_sem = rest[len(OFFSETS) :]
    load = start(field_ref, field, load_sem)
    wait(
        product_one(
            field, (r0, r1, r2, r3), weights_ref, inv_ref, col_ref, send_ref, term_ref, packs, scratch, [load]
        )
    )


def second_temporal(t_loc, arrived_ref, mix_ref, out_ref, columns, mixed, mix, arrived, load_sems, out_sems):
    wait([start(arrived_ref, arrived, load_sems.at[0]), start(mix_ref, mix, load_sems.at[1])])
    wait(mix_times(t_loc, mix[...], arrived, out_ref, columns, mixed, out_sems))


def rear_two(signal_ref, r0, r1, r2, r3, weights_ref, inv_ref, col_ref, term_ref, out_ref, *rest):
    *scratch, field, load_sem = rest
    load = start(signal_ref.at[field.shape[0] :], field, load_sem)
    wait(
        product_two(
            field, (r0, r1, r2, r3), weights_ref, inv_ref, col_ref, term_ref, lambda g: out_ref.at[g], scratch, [load]
        )
    )


def front_packs(early_ref, inv_ref, send_ref, *rest):
    packs = rest[: len(OFFSETS)]
    early, held, load_sem, pack_sems = rest[len(OFFSETS) :]
    start(early_ref, early, load_sem).wait()
    wait(pack(send_ref, early, inv_ref, packs, held, pack_sems))


def front_two(field_ref, r0, r1, r2, r3, weights_ref, inv_ref, col_ref, term_ref, _, out_ref, *rest):
    *scratch, field, load_sem = rest
    rows, width = field.shape[1:]

    def target(g):
        return out_ref.at[:rows, g * width : (g + 1) * width]

    load = start(field_ref, field, load_sem)
    wait(
        product_two(
            field, (r0, r1, r2, r3), weights_ref, inv_ref, col_ref, term_ref, target, scratch, [load]
        )
    )


def unblock(late_ref, out_ref, late, load_sem, sems):
    blocks, rows, width = late.shape
    start(late_ref, late, load_sem).wait()
    wait(
        [start(late.at[g], out_ref.at[rows:, g * width : (g + 1) * width], sems.at[g]) for g in range(blocks)]
    )


def swap(packs):
    count = lax.axis_size("dom")
    return [lax.ppermute(block, "dom", partners(i, count)) for i, block in enumerate(packs)]


def exchange(field):
    return lax.all_to_all(field, "tm", split_axis=0, concat_axis=0, tiled=True)


def body(signal, weights, send_list, col_ref, kernel, cheb_coef):
    probes, t_loc, n_loc = signal.shape
    blocks, per_row, width, _ = weights.shape
    rows = probes * t_loc // 2
    slots = send_list.shape[2]
    owners = lax.axis_size("tm")
    time = kernel.shape[1]
    ways = len(OFFSETS)
    pieces = rows // t_loc // 2
    xs = signal.reshape(2 * rows, n_loc)
    field = array(blocks, rows, width)
    packed = [(array(slots, rows, width), HBM)] * ways
    vm = pltpu.VMEM
    source = vm((blocks + ways * slots, rows, width), BF16)
    whole = vm((blocks, rows, width), BF16)
    held = vm((ways, slots, rows, width), BF16)
    columns = vm((time, rows // t_loc * width), BF16)
    square = vm((time, time), BF16)
    scratch_one = [source, whole, held, DMA((blocks,)), DMA((ways,))]
    scratch_two = [source, whole, whole, DMA((blocks,)), DMA]
    side_by_side = vm((rows, n_loc), BF16)
    work = 2 * rows * per_row * n_loc * width
    mixing = 2 * time * time * rows // t_loc * width

    def operands(x, packs, inv):
        received = [(r, VMEM) for r in swap(packs)]
        return [(x, HBM), *received, (weights, VMEM), (inv, VMEM), (col_ref, SMEM)]

    chunk = rows + time * t_loc // width
    (laid,) = call(
        lay_out,
        [(array(owners, chunk, width), HBM)],
        [(xs, HBM), (kernel, HBM)],
        [side_by_side, vm((owners, chunk, width), BF16), vm(kernel.shape, BF16), DMA((2,))],
    )
    arrived = exchange(laid)
    inv, *packs = call(
        first_scale,
        [(array(blocks + 8, width, dtype=F32), VMEM), *packed],
        [(xs, HBM), (weights, VMEM), (send_list, SMEM), (cheb_coef, SMEM)],
        [side_by_side, held, DMA((ways,)), DMA],
        flops=work // 8,
    )
    term, *packs, early, mix = call(
        functools.partial(rear_one, t_loc),
        [(field, HBM), *packed, (field, HBM), (array(time, time), HBM)],
        [*operands(xs, packs, inv), (send_list, SMEM), (arrived, HBM)],
        [*scratch_one, side_by_side, columns, whole, square, vm(laid.shape, BF16), DMA((3,)), DMA((pieces,))],
        flops=work + mixing,
    )
    early = exchange(early)
    takes = operands(xs, packs, inv)
    front = call(
        front_packs, packed, [(early, HBM), (inv, VMEM), (send_list, SMEM)], [whole, held, DMA, DMA((ways,))]
    )
    term, *front = lax.optimization_barrier((term, *front))
    (late,) = call(
        rear_two, [(field, HBM)], [*takes, (term, HBM)], [*scratch_two, side_by_side, DMA], flops=work
    )
    late, *front = lax.optimization_barrier((late, *front))
    late = exchange(late)
    takes = operands(early, front, inv)
    (late,) = call(
        functools.partial(second_temporal, t_loc),
        [(field, HBM)],
        [(late, HBM), (mix, HBM)],
        [columns, whole, square, whole, DMA((2,)), DMA((pieces,))],
        flops=mixing,
    )
    late, term = lax.optimization_barrier((late, takes[0][0]))
    takes[0] = (term, HBM)
    term, *packs = call(
        front_one, [(field, HBM), *packed], [*takes, (send_list, SMEM)], [*scratch_one, whole, DMA], flops=work
    )
    late, *packs = lax.optimization_barrier((late, *packs))
    late = exchange(late)
    takes = operands(early, packs, inv)
    out = array(2 * rows, n_loc)
    (rear,) = call(unblock, [(out, HBM)], [(late, HBM)], [whole, DMA, DMA((blocks,))])
    (out,) = call(
        front_two,
        [(out, HBM)],
        [*takes, (term, HBM), (rear, HBM)],
        [*scratch_two, whole, DMA],
        flops=work,
        aliases={9: 0},
    )
    return out.reshape(probes, t_loc, n_loc)


def solution(mesh):
    in_specs = (
        P(None, "tm", "dom"),
        P("dom", None, None, None),
        P("dom", None, None),
        P("dom", None),
        P("tm", None),
        P(),
    )
    out_specs = P(None, "tm", "dom")
    return jax.shard_map(body, mesh=mesh, in_specs=in_specs, out_specs=out_specs, check_vma=False)
```

```python
import functools

import jax
import jax.numpy as jnp
from jax import lax
from jax.experimental import pallas as pl
from jax.experimental.pallas import tpu as pltpu
from jax.sharding import PartitionSpec as P

REACH = 2
OFFSETS = tuple(range(-REACH, 0)) + tuple(range(1, REACH + 1))
F32, BF16 = jnp.float32, jnp.bfloat16
LIMIT = 24 * 2**20
SMEM = pl.BlockSpec(memory_space=pltpu.SMEM)
VMEM = pl.BlockSpec(memory_space=pltpu.VMEM)
HBM = pl.BlockSpec(memory_space=pltpu.HBM)
DMA = pltpu.SemaphoreType.DMA


def call(kernel, outs, ins, scratch, flops=0, aliases=None):
    arrays, specs = zip(*ins)
    shapes, results = zip(*outs)
    size = sum(a.size * a.dtype.itemsize for a in (*arrays, *shapes))
    arrays = [pltpu.with_memory_space_constraint(a, pltpu.HBM) if spec is HBM else a for a, spec in ins]
    shapes = [pltpu.HBM(a.shape, a.dtype) if spec is HBM else a for a, spec in outs]
    return pl.pallas_call(
        kernel,
        out_shape=shapes,
        in_specs=specs,
        out_specs=results,
        scratch_shapes=scratch,
        compiler_params=pltpu.CompilerParams(vmem_limit_bytes=LIMIT),
        cost_estimate=pl.CostEstimate(flops=flops, bytes_accessed=size, transcendentals=0),
        input_output_aliases=aliases or {},
    )(*arrays)


def array(*shape, dtype=BF16):
    return jax.ShapeDtypeStruct(shape, dtype)


def start(source, target, sem):
    copy = pltpu.make_async_copy(source, target, sem)
    copy.start()
    return copy


def wait(copies):
    for copy in copies:
        copy.wait()


def ended(g, count):
    size = count // 2
    return slice(g + 1 - size, g + 1) if (g + 1) % size == 0 else None


def times_transposed(a, b):
    return lax.dot_general(a, b, (((1,), (1,)), ((), ())), preferred_element_type=F32)


def block_of(ref, g, width):
    if len(ref.shape) == 3:
        return ref[g]
    at = g * width
    return ref[:, pl.ds(at if isinstance(g, int) else pl.multiple_of(at, width), width)]


def scaled_block(ref, inv_ref, g, width):
    return (block_of(ref, g, width).astype(F32) * inv_ref[pl.ds(g, 1), :]).astype(BF16)


def partner_ways():
    place = lax.axis_index("dom")
    return [0, 1, 2, 3]


def partners(index, count):
    return [(i, (i - OFFSETS[index]) % count) for i in range(count)]


def pack(send_ref, field_ref, inv_ref, packs, held, sems):
    width = inv_ref.shape[1]
    copies = []
    ways = partner_ways()
    for i, out in enumerate(packs):
        way = ways[i]
        for slot in range(out.shape[0]):
            held[i, slot] = scaled_block(field_ref, inv_ref, send_ref[0, way, slot], width)
        copies.append(start(held.at[i], out, sems.at[i]))
    return copies


def lay_out(signal_ref, kernel_ref, out_ref, field, held, mix, sems):
    owners, _, width = out_ref.shape
    t_loc, time = kernel_ref.shape
    rows = field.shape[0]
    mixing = start(kernel_ref, mix, sems.at[0])
    load = start(signal_ref.at[:rows], field, sems.at[1])
    mixing.wait()
    for i in range(owners):
        for q in range(time // width):
            held[i, rows + q * t_loc : rows + (q + 1) * t_loc] = mix[:, q * width : (q + 1) * width]
    load.wait()
    copies = []
    for i in range(owners):
        held[i, :rows] = field[:, i * width : (i + 1) * width]
        if part := ended(i, owners):
            copies.append(start(held.at[part], out_ref.at[part], sems.at[len(copies)]))
    wait(copies)


def first_scale(signal_ref, weights_ref, send_ref, coef_ref, inv_ref, *rest):
    *packs, field, held, sems, load_sem = rest
    blocks, per_row, width, _ = weights_ref.shape
    rows = field.shape[0]
    load = start(signal_ref.at[rows:], field, load_sem)
    ones = jnp.ones((16, width), BF16)
    for g in range(blocks):
        degree = times_transposed(ones, weights_ref[g, 0])
        for j in range(1, per_row):
            degree += times_transposed(ones, weights_ref[g, j])
        inv_ref[g : g + 1, :] = lax.rsqrt(degree[:1])
    for term in range(coef_ref.shape[0]):
        inv_ref[blocks + term : blocks + term + 1, :] = jnp.full((1, width), coef_ref[term], F32)
    load.wait()
    wait(pack(send_ref, field, inv_ref, packs, held, sems))


def place_received(blocks, received, source):
    for way, ref in zip(partner_ways(), received):
        slots = ref.shape[0]
        for slot in range(slots):
            source[blocks + way * slots + slot] = ref[slot]


def place_own(blocks, field_ref, inv_ref, source):
    for g in range(blocks):
        source[g] = scaled_block(field_ref, inv_ref, g, inv_ref.shape[1])


def block_product(g, col_ref, weights_ref, source):
    per_row = weights_ref.shape[1]
    picked = jnp.concatenate([source[col_ref[g, j]] for j in range(per_row)], axis=1)
    edges = jnp.concatenate([weights_ref[g, j] for j in range(per_row)], axis=1)
    return times_transposed(picked, edges)


def product_one(field, received, weights_ref, inv_ref, col_ref, send_ref, term_ref, packs, scratch, loads):
    source, term, held, sems, pack_sems = scratch
    blocks = weights_ref.shape[0]
    place_received(blocks, received, source)
    wait(loads)
    place_own(blocks, field, inv_ref, source)
    copies = []
    for g in range(blocks):
        total = block_product(g, col_ref, weights_ref, source)
        term[g] = (-inv_ref[g : g + 1, :] * total).astype(BF16)
        if part := ended(g, blocks):
            copies.append(start(term.at[part], term_ref.at[part], sems.at[len(copies)]))
    return copies + pack(send_ref, term, inv_ref, packs, held, pack_sems)


def product_two(field, received, weights_ref, inv_ref, col_ref, term_ref, target, scratch, loads):
    source, term, mixed, sems, term_sem = scratch
    start_term = start(term_ref, term, term_sem)
    blocks, _, width, _ = weights_ref.shape
    place_received(blocks, received, source)
    start_term.wait()
    place_own(blocks, term, inv_ref, source)
    coef = [inv_ref[blocks + i : blocks + i + 1, :] for i in range(3)]
    wait(loads)
    copies = []
    for g in range(blocks):
        total = block_product(g, col_ref, weights_ref, source)
        x = block_of(field, g, width).astype(F32)
        two = (-2.0 * inv_ref[g : g + 1, :] * total - x).astype(BF16).astype(F32)
        one = term[g].astype(F32)
        mixed[g] = (coef[0] * x + coef[1] * one + coef[2] * two).astype(BF16)
        copies += target(g, mixed, sems)
    return copies


def mix_times(t_loc, mix, field_ref, out_ref, columns, held, sems):
    owners, rows, width = out_ref.shape
    for p in range(rows // t_loc):
        part = slice(p * t_loc, (p + 1) * t_loc)
        for i in range(owners):
            columns[i * t_loc : (i + 1) * t_loc, p * width : (p + 1) * width] = field_ref[i, part]
    step = 2 * width
    pieces = columns.shape[1] // step
    depth = rows // pieces
    copies = []
    for c in range(pieces):
        out = jnp.dot(mix, columns[:, c * step : (c + 1) * step], preferred_element_type=F32).astype(BF16)
        for q in range(step // width):
            at = c * depth + q * t_loc
            for i in range(owners):
                held[i, at : at + t_loc] = out[i * t_loc : (i + 1) * t_loc, q * width : (q + 1) * width]
        part = slice(c * depth, (c + 1) * depth)
        copies.append(start(held.at[:, part], out_ref.at[:, part], sems.at[c]))
    return copies


def rear_one(t_loc, signal_ref, r0, r1, r2, r3, weights_ref, inv_ref, col_ref, send_ref, arrived_ref, term_ref, *rest):
    *packs, out_ref, mix_ref = rest[: len(OFFSETS) + 2]
    *scratch, field, columns, mixed, mix, arrived, load_sems, out_sems = rest[len(OFFSETS) + 2 :]
    owners, rows, width = out_ref.shape
    load = start(signal_ref.at[rows:], field, load_sems.at[0])
    load_arrived = start(arrived_ref, arrived, load_sems.at[2])
    copies = product_one(
        field, (r0, r1, r2, r3), weights_ref, inv_ref, col_ref, send_ref, term_ref, packs, scratch, [load]
    )
    load_arrived.wait()
    for i in range(owners):
        for q in range(mix.shape[1] // width):
            mix[i * t_loc : (i + 1) * t_loc, q * width : (q + 1) * width] = arrived[
                i, rows + q * t_loc : rows + (q + 1) * t_loc
            ]
    copies.append(start(mix, mix_ref, load_sems.at[1]))
    wait(copies + mix_times(t_loc, mix[...], arrived, out_ref, columns, mixed, out_sems))


def front_one(field_ref, r0, r1, r2, r3, weights_ref, inv_ref, col_ref, send_ref, term_ref, *rest):
    packs = rest[: len(OFFSETS)]
    *scratch, field, load_sem = rest[len(OFFSETS) :]
    load = start(field_ref, field, load_sem)
    wait(
        product_one(
            field, (r0, r1, r2, r3), weights_ref, inv_ref, col_ref, send_ref, term_ref, packs, scratch, [load]
        )
    )


def second_temporal(t_loc, arrived_ref, mix_ref, out_ref, columns, mixed, mix, arrived, load_sems, out_sems):
    wait([start(arrived_ref, arrived, load_sems.at[0]), start(mix_ref, mix, load_sems.at[1])])
    wait(mix_times(t_loc, mix[...], arrived, out_ref, columns, mixed, out_sems))


def rear_two(signal_ref, r0, r1, r2, r3, weights_ref, inv_ref, col_ref, term_ref, out_ref, *rest):
    *scratch, field, load_sem = rest
    load = start(signal_ref.at[field.shape[0] :], field, load_sem)

    def target(g, mixed, sems):
        part = ended(g, mixed.shape[0])
        return [start(mixed.at[part], out_ref.at[part], sems.at[g])] if part else []

    wait(
        product_two(
            field, (r0, r1, r2, r3), weights_ref, inv_ref, col_ref, term_ref, target, scratch, [load]
        )
    )


def front_packs(early_ref, inv_ref, send_ref, *rest):
    packs = rest[: len(OFFSETS)]
    early, held, load_sem, pack_sems = rest[len(OFFSETS) :]
    start(early_ref, early, load_sem).wait()
    wait(pack(send_ref, early, inv_ref, packs, held, pack_sems))


def front_two(field_ref, r0, r1, r2, r3, weights_ref, inv_ref, col_ref, term_ref, _, out_ref, *rest):
    *scratch, field, load_sem = rest
    rows, width = field.shape[1:]

    def target(g, mixed, sems):
        return [start(mixed.at[g], out_ref.at[:rows, g * width : (g + 1) * width], sems.at[g])]

    load = start(field_ref, field, load_sem)
    wait(
        product_two(
            field, (r0, r1, r2, r3), weights_ref, inv_ref, col_ref, term_ref, target, scratch, [load]
        )
    )


def unblock(late_ref, out_ref, late, load_sem, sems):
    blocks, rows, width = late.shape
    start(late_ref, late, load_sem).wait()
    wait(
        [start(late.at[g], out_ref.at[rows:, g * width : (g + 1) * width], sems.at[g]) for g in range(blocks)]
    )


def swap(packs):
    count = lax.axis_size("dom")
    return [lax.ppermute(block, "dom", partners(i, count)) for i, block in enumerate(packs)]


def exchange(field):
    return lax.all_to_all(field, "tm", split_axis=0, concat_axis=0, tiled=True)


def body(signal, weights, send_list, col_ref, kernel, cheb_coef):
    probes, t_loc, n_loc = signal.shape
    blocks, per_row, width, _ = weights.shape
    rows = probes * t_loc // 2
    slots = send_list.shape[2]
    owners = lax.axis_size("tm")
    time = kernel.shape[1]
    ways = len(OFFSETS)
    pieces = rows // t_loc // 2
    xs = signal.reshape(2 * rows, n_loc)
    field = array(blocks, rows, width)
    packed = [(array(slots, rows, width), HBM)] * ways
    vm = pltpu.VMEM
    source = vm((blocks + ways * slots, rows, width), BF16)
    whole = vm((blocks, rows, width), BF16)
    held = vm((ways, slots, rows, width), BF16)
    columns = vm((time, rows // t_loc * width), BF16)
    square = vm((time, time), BF16)
    scratch_one = [source, whole, held, DMA((blocks,)), DMA((ways,))]
    scratch_two = [source, whole, whole, DMA((blocks,)), DMA]
    side_by_side = vm((rows, n_loc), BF16)
    work = 2 * rows * per_row * n_loc * width
    mixing = 2 * time * time * rows // t_loc * width

    def operands(x, packs, inv):
        received = [(r, VMEM) for r in swap(packs)]
        return [(x, HBM), *received, (weights, VMEM), (inv, VMEM), (col_ref, SMEM)]

    chunk = rows + time * t_loc // width
    (laid,) = call(
        lay_out,
        [(array(owners, chunk, width), HBM)],
        [(xs, HBM), (kernel, HBM)],
        [side_by_side, vm((owners, chunk, width), BF16), vm(kernel.shape, BF16), DMA((2,))],
    )
    arrived = exchange(laid)
    inv, *packs = call(
        first_scale,
        [(array(blocks + 8, width, dtype=F32), VMEM), *packed],
        [(xs, HBM), (weights, VMEM), (send_list, SMEM), (cheb_coef, SMEM)],
        [side_by_side, held, DMA((ways,)), DMA],
        flops=work // 8,
    )
    term, *packs, early, mix = call(
        functools.partial(rear_one, t_loc),
        [(field, HBM), *packed, (field, HBM), (array(time, time), HBM)],
        [*operands(xs, packs, inv), (send_list, SMEM), (arrived, HBM)],
        [*scratch_one, side_by_side, columns, whole, square, vm(laid.shape, BF16), DMA((3,)), DMA((pieces,))],
        flops=work + mixing,
    )
    early = exchange(early)
    takes = operands(xs, packs, inv)
    front = call(
        front_packs, packed, [(early, HBM), (inv, VMEM), (send_list, SMEM)], [whole, held, DMA, DMA((ways,))]
    )
    term, *front = lax.optimization_barrier((term, *front))
    (late,) = call(
        rear_two, [(field, HBM)], [*takes, (term, HBM)], [*scratch_two, side_by_side, DMA], flops=work
    )
    late, *front = lax.optimization_barrier((late, *front))
    late = exchange(late)
    takes = operands(early, front, inv)
    (late,) = call(
        functools.partial(second_temporal, t_loc),
        [(field, HBM)],
        [(late, HBM), (mix, HBM)],
        [columns, whole, square, whole, DMA((2,)), DMA((pieces,))],
        flops=mixing,
    )
    late, term = lax.optimization_barrier((late, takes[0][0]))
    takes[0] = (term, HBM)
    term, *packs = call(
        front_one, [(field, HBM), *packed], [*takes, (send_list, SMEM)], [*scratch_one, whole, DMA], flops=work
    )
    late, *packs = lax.optimization_barrier((late, *packs))
    late = exchange(late)
    takes = operands(early, packs, inv)
    out = array(2 * rows, n_loc)
    (rear,) = call(unblock, [(out, HBM)], [(late, HBM)], [whole, DMA, DMA((blocks,))])
    (out,) = call(
        front_two,
        [(out, HBM)],
        [*takes, (term, HBM), (rear, HBM)],
        [*scratch_two, whole, DMA],
        flops=work,
        aliases={9: 0},
    )
    return out.reshape(probes, t_loc, n_loc)


def solution(mesh):
    in_specs = (
        P(None, "tm", "dom"),
        P("dom", None, None, None),
        P("dom", None, None),
        P("dom", None),
        P("tm", None),
        P(),
    )
    out_specs = P(None, "tm", "dom")
    return jax.shard_map(body, mesh=mesh, in_specs=in_specs, out_specs=out_specs, check_vma=False)
```
